32 devices in a mesh: shard: 8 (over y, x, core), context: 4 (over z).
Axes of the slice: x: 2, y: 2, z: 4, core: 2. Of those that a mesh axis runs over, the one named last changes fastest.
Arguments:
- block_input: float32 [8192, 2048], P(('shard', 'context')), may hold values from -6 to 6
- input_weight: bfloat16 [2048, 14336], P('shard')
- input_bias: bfloat16 [14336], P('shard'), may hold values from -3 to 3
- output_weight: bfloat16 [10240, 2048], P('shard')
- output_bias: bfloat16 [2, 2048], P(None, 'shard'), may hold values from -3 to 3
- norm_gain: bfloat16 [2048], P('shard'), may hold values from 0.5 to 1.5
- norm_bias: bfloat16 [2048], P('shard'), may hold values from -2 to 2
- assignment: int32 [8], replicated, may hold values from 0 to 7, as said below
- positions: int32 [8192], P(('shard', 'context')), may hold values from 0 to 2046, as said below
- cotangent: float32 [8192, 2048], P(('shard', 'context')), may hold values from -6 to 6
Outputs:
- block_output: float32 [8192, 2048], P(('shard', 'context'))
- block_input_gradient: float32 [8192, 2048], P(('shard', 'context'))
- input_weight_gradient: float32 [2048, 14336], P('shard')
- input_bias_gradient: float32 [14336], P('shard')
- output_weight_gradient: float32 [10240, 2048], P('shard')
- output_bias_gradient: float32 [2, 2048], P(None, 'shard')
- norm_gain_gradient: float32 [2048], P('shard')
- norm_bias_gradient: float32 [2048], P('shard')
The draws below stay inside these ranges and needn't reach their ends.
Inputs may be any that keep to these rules, and one draw needn't show every extreme that they name: `assignment`: a permutation: each of 0 to 7 once, the same for every context group. `positions`: within a sequence, a token's position is the sequence's start offset (0 to 1023) plus its causal index inside the sequence.
All inputs are finite; a program needn't handle non-finite values.
Results may differ from the reference program's by a relative error of at most 0.015.
Values may be sent and summed in bfloat16 or wider, within the bound.
No kernel may reach another device: no remote copies, remote signals or barrier semaphores. Data moves between devices by JAX's collectives and lax.ppermute only.
A program may use at most 640 MiB of HBM per device.

```python
import math
import jax
import jax.numpy as jnp
from jax import lax

D = 2048
FF = 8192
HEADS = 32
HEAD_DIM = 64
ROT = 32
SEQ_LEN = 1024
TOK_DEV = 256
GROUP = 1024
BLK = 128
BLOCKS = 8
TOKENS = 8192
N_CONTEXT = 4


def order_table(key):
    return jax.random.permutation(jax.random.fold_in(key, 11), BLOCKS).astype(jnp.int32)


def draw_assignment(key, part):
    return order_table(key)


def draw_positions(key, part):
    table = order_table(key)
    row_index = jnp.arange(TOKENS, dtype=jnp.int32)
    local_row = row_index % GROUP
    causal = table[local_row // BLK] * BLK + local_row % BLK
    sequence_id = row_index // GROUP * (GROUP // SEQ_LEN) + causal // SEQ_LEN
    starts = jax.random.randint(jax.random.fold_in(key, 13), (TOKENS // SEQ_LEN,), 0, SEQ_LEN).astype(jnp.int32)
    starts = starts.at[0].set(SEQ_LEN - 1).at[-1].set(0)
    return (starts[sequence_id] + causal % SEQ_LEN).astype(jnp.int32)


def draw_input_weight(key, part):
    key = jax.random.fold_in(key, 3)
    base = jax.random.normal(key, (D, 3 * D + FF), jnp.float32) * D ** (-0.5)
    column = jnp.arange(3 * D + FF)
    factor = jnp.where(column < 2 * D, 1.5, 1.0)
    return (base * factor[None, :]).astype(jnp.bfloat16)


def draw_output_weight(key, part):
    key = jax.random.fold_in(key, 5)
    base = jax.random.normal(key, (D + FF, D), jnp.float32)
    row_index = jnp.arange(D + FF)
    factor = jnp.where(row_index < D, 6.0 * D ** (-0.5), 1.5 * FF ** (-0.5))
    return (base * factor[:, None]).astype(jnp.bfloat16)


def shard_levels(own_key, shape, cuts, least, largest):
    def one(axis_at, blocks):
        steps = jax.random.uniform(jax.random.fold_in(jax.random.fold_in(own_key, 6), axis_at), (blocks,), jnp.float32, least / len(cuts), largest / len(cuts))
        return jnp.repeat(jnp.exp(steps), shape[axis_at] // blocks).reshape((-1,) + (1,) * (len(shape) - axis_at - 1))

    factor_of = one(*cuts[0])
    for cut in cuts[1:]:
        factor_of = factor_of * one(*cut)
    return factor_of


def gaussian(own_key, shape, width, limit, shards=(), held_as=jnp.bfloat16):
    drawn = width * jax.random.normal(own_key, shape, jnp.float32)
    if shards:
        drawn = drawn * shard_levels(own_key, shape, shards, -0.22, 0.18)
    return jnp.clip(drawn, -limit, limit).astype(held_as)


def setup_inputs(seed: int = 0) -> dict:
    key_of = jax.random.split(jax.random.key(seed), 11)
    block_input = gaussian(key_of[0], (TOKENS, D), 1.0, 6.0, ((0, 32),), jnp.float32)
    input_weight = draw_input_weight(jax.random.fold_in(key_of[10], 71), 0)
    input_bias = gaussian(key_of[2], (3 * D + FF,), 0.5, 3.0, ((0, 8),))
    output_weight = draw_output_weight(jax.random.fold_in(key_of[10], 71), 0)
    output_bias = gaussian(key_of[4], (2, D), 0.5, 3.0, ((1, 8),))
    norm_gain = jnp.clip(1.0 + 0.1 * jax.random.normal(key_of[5], (D,), jnp.float32), 0.5, 1.5).astype(jnp.bfloat16)
    norm_bias = gaussian(key_of[6], (D,), 0.3, 2.0, ((0, 8),))
    assignment = draw_assignment(jax.random.fold_in(key_of[10], 71), 0)
    positions = draw_positions(jax.random.fold_in(key_of[10], 71), 0)
    cotangent = gaussian(key_of[9], (TOKENS, D), 1.0, 6.0, ((0, 32),), jnp.float32)
    return dict(block_input=block_input, input_weight=input_weight, input_bias=input_bias, output_weight=output_weight, output_bias=output_bias, norm_gain=norm_gain, norm_bias=norm_bias, assignment=assignment, positions=positions, cotangent=cotangent)


epsilon = 1e-05
floor_score = -1e+30

def causal_index(row_index, assignment, half_rows):
    block_index = row_index // half_rows
    matches = block_index[:, None] == jnp.arange(assignment.shape[0], dtype=jnp.int32)[None, :]
    chosen = lax.optimization_barrier(jnp.sum(jnp.where(matches, assignment[None, :], 0), axis=1)).astype(jnp.int32)
    return chosen * half_rows + row_index % half_rows

def rotary_tables(position_ids):
    half_rot = ROT // 2
    frequency = 10000.0 ** (-2.0 * jnp.arange(half_rot, dtype=jnp.float32) / ROT)
    angles = position_ids.astype(jnp.float32)[:, None] * frequency[None, :]
    return (jnp.cos(angles), jnp.sin(angles))

def rotate(field, cosine_table, sine_table, direction):
    half_rot = ROT // 2
    first_half = field[..., :half_rot]
    second_half = field[..., half_rot:ROT]
    remainder = field[..., ROT:]
    cosine = cosine_table[:, None, :]
    sine_part = sine_table[:, None, :] * direction
    return jnp.concatenate([first_half * cosine - second_half * sine_part, second_half * cosine + first_half * sine_part, remainder], axis=-1)

def widen(array):
    return array.astype(jnp.float32)

def gelu_tanh(value):
    return jax.nn.gelu(value, approximate=True)

def attend(query, keys, values, allowed, heads_per):
    query_count, head_count, head_size = query.shape
    scaling = head_size ** (-0.5)

    def head_step(group_index, carry):
        output, log_total = carry
        first_head = group_index * heads_per
        query_part = lax.dynamic_slice_in_dim(query, first_head, heads_per, 1)
        key_part = lax.dynamic_slice_in_dim(keys, first_head, heads_per, 1)
        value_part = lax.dynamic_slice_in_dim(values, first_head, heads_per, 1)
        scores = jnp.einsum('qhd,khd->hqk', widen(query_part), widen(key_part)) * scaling
        scores = jnp.where(allowed[None], scores, floor_score)
        highest = lax.optimization_barrier(jnp.max(scores, axis=2, keepdims=True))
        part_total = highest + jnp.log(lax.optimization_barrier(jnp.sum(jnp.exp(scores - highest), axis=2, keepdims=True)))
        rounded = jnp.exp(scores - part_total).astype(jnp.bfloat16)
        mixture = jnp.einsum('hqk,khd->qhd', widen(rounded), widen(value_part))
        output = lax.dynamic_update_slice_in_dim(output, mixture.astype(jnp.bfloat16), first_head, 1)
        log_total = lax.dynamic_update_slice_in_dim(log_total, part_total[:, :, 0], first_head, 0)
        return (output, log_total)
    initial = (jnp.zeros((query_count, head_count, head_size), jnp.bfloat16), jnp.zeros((head_count, query_count), jnp.float32))
    return lax.fori_loop(0, head_count // heads_per, head_step, initial)

def attend_back(query, keys, values, allowed, log_total, upstream, delta, heads_per):
    query_count, head_count, head_size = query.shape
    key_count = keys.shape[0]
    scaling = head_size ** (-0.5)

    def head_step(group_index, carry):
        query_total, key_total, value_total = carry
        first_head = group_index * heads_per
        query_part = lax.dynamic_slice_in_dim(query, first_head, heads_per, 1)
        key_part = lax.dynamic_slice_in_dim(keys, first_head, heads_per, 1)
        value_part = lax.dynamic_slice_in_dim(values, first_head, heads_per, 1)
        upstream_part = lax.dynamic_slice_in_dim(upstream, first_head, heads_per, 1)
        total_part = lax.dynamic_slice_in_dim(log_total, first_head, heads_per, 0)
        delta_part = lax.dynamic_slice_in_dim(delta, first_head, heads_per, 0)
        scores = jnp.einsum('qhd,khd->hqk', widen(query_part), widen(key_part)) * scaling
        scores = jnp.where(allowed[None], scores, floor_score)
        weights = jnp.exp(scores - total_part[:, :, None])
        rounded = weights.astype(jnp.bfloat16)
        value_term = jnp.einsum('hqk,qhd->khd', widen(rounded), widen(upstream_part))
        weight_slope = jnp.einsum('qhd,khd->hqk', widen(upstream_part), widen(value_part))
        score_grad = (weights * (weight_slope - delta_part[:, :, None])).astype(jnp.bfloat16)
        query_term = jnp.einsum('hqk,khd->qhd', widen(score_grad), widen(key_part)) * scaling
        key_term = jnp.einsum('hqk,qhd->khd', widen(score_grad), widen(query_part)) * scaling
        query_total = lax.dynamic_update_slice_in_dim(query_total, query_term, first_head, 1)
        key_total = lax.dynamic_update_slice_in_dim(key_total, key_term, first_head, 1)
        value_total = lax.dynamic_update_slice_in_dim(value_total, value_term, first_head, 1)
        return (query_total, key_total, value_total)
    initial = (jnp.zeros((query_count, head_count, head_size), jnp.float32), jnp.zeros((key_count, head_count, head_size), jnp.float32), jnp.zeros((key_count, head_count, head_size), jnp.float32))
    return lax.fori_loop(0, head_count // heads_per, head_step, initial)

def reference(block_input, input_weight, input_bias, output_weight, output_bias, norm_gain, norm_bias, assignment, positions, cotangent):
    group = TOK_DEV * N_CONTEXT
    half_rows = TOK_DEV // 2
    group_count = block_input.shape[0] // group
    heads_per = math.gcd(HEADS, 8)
    causal = causal_index(jnp.arange(group, dtype=jnp.int32), assignment, half_rows)
    allowed = (causal[None, :] <= causal[:, None]) & (causal[None, :] // SEQ_LEN == causal[:, None] // SEQ_LEN)
    gain = norm_gain.astype(jnp.float32)
    shift = norm_bias.astype(jnp.float32)
    bias_sum = output_bias[0].astype(jnp.float32) + output_bias[1].astype(jnp.float32)
    in_bias = input_bias.astype(jnp.float32)

    def one_group(carry, inputs):
        weight_in_sum, bias_in_sum, weight_out_sum, bias_out_sum, gain_sum, shift_sum = carry
        group_input, group_positions, group_cotangent = inputs
        centred = group_input - lax.optimization_barrier(jnp.mean(group_input, axis=1, keepdims=True))
        inverse_std = lax.rsqrt(lax.optimization_barrier(jnp.mean(centred * centred, axis=1, keepdims=True)) + epsilon)
        normalized = centred * inverse_std
        normed = (normalized * gain + shift).astype(jnp.bfloat16)
        projected = jnp.dot(normed, input_weight, preferred_element_type=jnp.float32) + in_bias
        cosine_table, sine_table = rotary_tables(group_positions)
        query = rotate(projected[:, :D].reshape(group, HEADS, HEAD_DIM), cosine_table, sine_table, 1.0).astype(jnp.bfloat16)
        keys = rotate(projected[:, D:2 * D].reshape(group, HEADS, HEAD_DIM), cosine_table, sine_table, 1.0).astype(jnp.bfloat16)
        values = projected[:, 2 * D:3 * D].astype(jnp.bfloat16).reshape(group, HEADS, HEAD_DIM)
        hidden_pre = projected[:, 3 * D:]
        activation = gelu_tanh(hidden_pre).astype(jnp.bfloat16)
        attended, log_total = attend(query, keys, values, allowed, heads_per)
        joined = jnp.concatenate([attended.reshape(group, D), activation], axis=1)
        group_output = group_input + jnp.dot(joined, output_weight, preferred_element_type=jnp.float32) + bias_sum
        upstream = group_cotangent.astype(jnp.bfloat16)
        joined_grad = jnp.dot(upstream, output_weight.T, preferred_element_type=jnp.float32)
        attended_grad = joined_grad[:, :D].astype(jnp.bfloat16).reshape(group, HEADS, HEAD_DIM)
        hidden_grad = jax.vjp(gelu_tanh, hidden_pre)[1](joined_grad[:, D:])[0]
        delta = lax.optimization_barrier(jnp.sum(widen(attended_grad) * widen(attended), axis=2)).T
        query_total, key_total, value_total = attend_back(query, keys, values, allowed, log_total, attended_grad, delta, heads_per)
        query_total = rotate(query_total, cosine_table, sine_table, -1.0).reshape(group, D)
        key_total = rotate(key_total, cosine_table, sine_table, -1.0).reshape(group, D)
        projected_grad = jnp.concatenate([query_total, key_total, value_total.reshape(group, D), hidden_grad], axis=1)
        rounded_grad = projected_grad.astype(jnp.bfloat16)
        normed_grad = jnp.dot(rounded_grad, input_weight.T, preferred_element_type=jnp.float32)
        weight_in_sum = weight_in_sum + jnp.dot(normed.T, rounded_grad, preferred_element_type=jnp.float32)
        weight_out_sum = weight_out_sum + jnp.dot(joined.T, upstream, preferred_element_type=jnp.float32)
        bias_in_sum = bias_in_sum + lax.optimization_barrier(jnp.sum(projected_grad, axis=0))
        bias_out_sum = bias_out_sum + lax.optimization_barrier(jnp.sum(group_cotangent, axis=0))
        gain_sum = gain_sum + lax.optimization_barrier(jnp.sum(normed_grad * normalized, axis=0))
        shift_sum = shift_sum + lax.optimization_barrier(jnp.sum(normed_grad, axis=0))
        scaled = normed_grad * gain
        input_grad = group_cotangent + inverse_std * (scaled - lax.optimization_barrier(jnp.mean(scaled, axis=1, keepdims=True)) - normalized * lax.optimization_barrier(jnp.mean(scaled * normalized, axis=1, keepdims=True)))
        return ((weight_in_sum, bias_in_sum, weight_out_sum, bias_out_sum, gain_sum, shift_sum), (group_output, input_grad))
    initial = (jnp.zeros((D, 3 * D + FF), jnp.float32), jnp.zeros((3 * D + FF,), jnp.float32), jnp.zeros((D + FF, D), jnp.float32), jnp.zeros((D,), jnp.float32), jnp.zeros((D,), jnp.float32), jnp.zeros((D,), jnp.float32))
    stacked = (block_input.reshape(group_count, group, D), positions.reshape(group_count, group), cotangent.reshape(group_count, group, D))
    sums, (outputs, gradients) = lax.scan(one_group, initial, stacked)
    weight_in_sum, bias_in_sum, weight_out_sum, bias_out_sum, gain_sum, shift_sum = sums
    total_rows = block_input.shape[0]
    return (outputs.reshape(total_rows, D), gradients.reshape(total_rows, D), weight_in_sum, bias_in_sum, weight_out_sum, jnp.stack([bias_out_sum, bias_out_sum]), gain_sum, shift_sum)
```

```python
import functools

import jax
import jax.numpy as jnp
from jax import lax
from jax.experimental import pallas as pl
from jax.experimental.pallas import tpu as pltpu
from jax.sharding import PartitionSpec as P

D = 2048
FF = 8192
HEADS = 32
HEAD_DIM = 64
ROT = 32
SEQ_LEN = 1024
BLK = 128
TILE = 256

epsilon = 1e-05
floor_score = -1e30

F32 = jnp.float32
BF16 = jnp.bfloat16


def dot(a, b, dims=((1,), (0,))):
    return lax.dot_general(a, b, (dims, ((), ())), preferred_element_type=F32)


def column_plan(shard_size, context_size):
    rows = (D + FF) // shard_size
    blocks = rows // HEAD_DIM
    split = HEADS % blocks
    if rows % HEAD_DIM == 0 and split % context_size == 0 and (blocks - split) % context_size == 0:
        inner = [
            (at * HEAD_DIM, size * HEAD_DIM // context_size)
            for at, size in ((0, split), (split, blocks - split))
            if size
        ]
        segments = [(s * rows + at, width) for s in range(shard_size) for at, width in inner]
        return inner, segments
    return None, [(0, D // context_size), (D, FF // context_size)]


def take(array, segments, context, axis):
    parts = [
        lax.dynamic_slice_in_dim(array, base + context * width, width, axis)
        for base, width in segments
    ]
    return jnp.concatenate(parts, axis) if len(parts) > 1 else parts[0]


def untake(gathered, segments, axis):
    parts = []
    at = 0
    for _, width in segments:
        for c in range(gathered.shape[0]):
            parts.append(lax.slice_in_dim(gathered[c], at, at + width, axis=axis))
        at += width
    return jnp.concatenate(parts, axis)


def lane_mask(shape, head):
    lane = lax.broadcasted_iota(jnp.int32, shape, len(shape) - 1)
    return (lane // HEAD_DIM) == head


def rotated(x, cosine, sine_low, sine_high):
    half = ROT // 2
    width = x.shape[1]
    return (
        x * cosine
        + pltpu.roll(x, width - half, 1) * sine_low
        + pltpu.roll(x, half, 1) * sine_high
    )


def stored(place_ref, p):
    return pl.ds(pl.multiple_of(place_ref[p] * BLK, BLK), BLK)


def attend_kernel(
    place_ref, q_ref, k_ref, v_ref, cos_ref, low_ref, high_ref,
    out_ref, total_ref, qr_ref, kr_ref, vr_ref,
):
    tokens = q_ref.shape[0]
    for p in range(tokens // BLK):
        here = pl.ds(p * BLK, BLK)
        there = stored(place_ref, p)
        cosine, low, high = cos_ref[there, :], low_ref[there, :], high_ref[there, :]
        query = rotated(q_ref[there, :], cosine, low, high).astype(BF16)
        qr_ref[here, :] = (query.astype(F32) * HEAD_DIM**-0.5).astype(BF16)
        kr_ref[here, :] = rotated(k_ref[there, :], cosine, low, high).astype(BF16)
        vr_ref[here, :] = v_ref[there, :].astype(BF16)
    for tile in range(tokens // TILE):
        first = tile * TILE // SEQ_LEN * SEQ_LEN
        last = (tile + 1) * TILE
        count = last - first
        query = qr_ref[pl.ds(tile * TILE, TILE), :]
        keys = kr_ref[pl.ds(first, count), :]
        values = vr_ref[pl.ds(first, count), :]
        row = lax.broadcasted_iota(jnp.int32, (TILE, count), 0) + (tile * TILE - first)
        allowed = lax.broadcasted_iota(jnp.int32, (TILE, count), 1) <= row
        outs, totals = [], []
        for head in range(2):
            mine = jnp.where(lane_mask(query.shape, head), query, jnp.zeros_like(query))
            scores = jnp.where(allowed, dot(mine, keys, ((1,), (1,))), floor_score)
            highest = jnp.max(scores, axis=1, keepdims=True)
            weights = jnp.exp(scores - highest)
            total = jnp.sum(weights, axis=1, keepdims=True)
            outs.append(dot(weights.astype(BF16), values) / total)
            totals.append(highest + jnp.log(total))
        wide = (TILE, 2 * HEAD_DIM)
        first_head = lane_mask(wide, 0)
        out = jnp.where(first_head, outs[0], outs[1]).astype(BF16)
        total_ref[pl.ds(tile * TILE, TILE), :] = jnp.where(
            first_head, jnp.broadcast_to(totals[0], wide), jnp.broadcast_to(totals[1], wide)
        )
        for part in range(TILE // BLK):
            out_ref[stored(place_ref, tile * (TILE // BLK) + part), :] = out[
                part * BLK : (part + 1) * BLK
            ]


def attend_back_kernel(
    place_ref, q_ref, k_ref, v_ref, total_ref, out_ref, grad_ref, cos_ref, low_ref, high_ref,
    dq_ref, dk_ref, dv_ref, sums_ref, dq_acc, dk_acc, dv_acc,
):
    tokens = q_ref.shape[0]
    blocks = TILE // BLK
    dk_acc[...] = jnp.zeros_like(dk_acc)
    dv_acc[...] = jnp.zeros_like(dv_acc)
    for tile in range(tokens // TILE):
        first = tile * TILE // SEQ_LEN * SEQ_LEN
        last = (tile + 1) * TILE
        count = last - first
        places = [stored(place_ref, tile * blocks + part) for part in range(blocks)]
        query = q_ref[pl.ds(tile * TILE, TILE), :]
        keys = k_ref[pl.ds(first, count), :]
        values = v_ref[pl.ds(first, count), :]
        grad = jnp.concatenate([grad_ref[place, :] for place in places], 0)
        out = jnp.concatenate([out_ref[place, :] for place in places], 0)
        product = grad.astype(F32) * out.astype(F32)
        row = lax.broadcasted_iota(jnp.int32, (TILE, count), 0) + (tile * TILE - first)
        allowed = lax.broadcasted_iota(jnp.int32, (TILE, count), 1) <= row
        dq = jnp.zeros((TILE, 2 * HEAD_DIM), F32)
        for head in range(2):
            narrow = lane_mask(query.shape, head)
            mine = jnp.where(narrow, query, jnp.zeros_like(query))
            grad_mine = jnp.where(narrow, grad, jnp.zeros_like(grad))
            delta = jnp.sum(jnp.where(narrow, product, 0.0), axis=1, keepdims=True)
            total = total_ref[pl.ds(tile * TILE, TILE), pl.ds(head * HEAD_DIM, 1)]
            scores = jnp.where(allowed, dot(mine, keys, ((1,), (1,))), floor_score)
            weights = jnp.exp(scores - total)
            slope = dot(grad_mine, values, ((1,), (1,)))
            score_grad = (weights * (slope - delta)).astype(BF16)
            rounded = weights.astype(BF16)
            keys_mine = jnp.where(
                lane_mask(keys.shape, head), keys, jnp.zeros_like(keys)
            )
            dq = dq + dot(score_grad, keys_mine)
            dk_acc[pl.ds(first, count), :] += dot(score_grad, mine, ((0,), (0,)))
            dv_acc[pl.ds(first, count), :] += dot(rounded, grad_mine, ((0,), (0,)))
        dq_acc[pl.ds(tile * TILE, TILE), :] = dq * HEAD_DIM**-0.5
    sums = [jnp.zeros((1, 2 * HEAD_DIM), F32) for _ in range(3)]
    for p in range(tokens // BLK):
        here = pl.ds(p * BLK, BLK)
        there = stored(place_ref, p)
        cosine, low, high = cos_ref[there, :], -low_ref[there, :], -high_ref[there, :]
        for i, (acc, ref) in enumerate(((dq_acc, dq_ref), (dk_acc, dk_ref), (dv_acc, dv_ref))):
            part = acc[here, :]
            if i < 2:
                part = rotated(part, cosine, low, high)
            sums[i] = sums[i] + jnp.sum(part, axis=0, keepdims=True)
            ref[there, :] = part.astype(BF16)
    zero = jnp.zeros((5, 2 * HEAD_DIM), F32)
    sums_ref[...] = jnp.concatenate(sums + [zero], 0)


def attend(place, projected, tables, heads):
    tokens = projected.shape[0]
    pairs = heads // 2
    wide = 2 * HEAD_DIM

    def block(offset):
        return pl.BlockSpec((tokens, wide), lambda h, place: (0, h + offset))

    table = pl.BlockSpec((tokens, wide), lambda h, place: (0, 0))
    shape = (tokens, heads * HEAD_DIM)
    return pl.pallas_call(
        attend_kernel,
        grid_spec=pltpu.PrefetchScalarGridSpec(
            num_scalar_prefetch=1,
            grid=(pairs,),
            in_specs=[block(0), block(pairs), block(2 * pairs), table, table, table],
            out_specs=[block(0)] * 5,
        ),
        out_shape=[
            jax.ShapeDtypeStruct(shape, BF16),
            jax.ShapeDtypeStruct(shape, F32),
            jax.ShapeDtypeStruct(shape, BF16),
            jax.ShapeDtypeStruct(shape, BF16),
            jax.ShapeDtypeStruct(shape, BF16),
        ],
        compiler_params=pltpu.CompilerParams(vmem_limit_bytes=48 * 2**20),
        cost_estimate=pl.CostEstimate(
            flops=8 * tokens * tokens * wide * pairs, bytes_accessed=30 * tokens * wide * pairs,
            transcendentals=tokens * tokens * heads,
        ),
    )(place, projected, projected, projected, *tables)


def attend_back(place, query, keys, values, total, out, grad, tables, heads):
    tokens = query.shape[0]
    pairs = heads // 2
    wide = 2 * HEAD_DIM
    block = pl.BlockSpec((tokens, wide), lambda h, place: (0, h))
    table = pl.BlockSpec((tokens, wide), lambda h, place: (0, 0))
    shape = jax.ShapeDtypeStruct((tokens, heads * HEAD_DIM), BF16)
    return pl.pallas_call(
        attend_back_kernel,
        grid_spec=pltpu.PrefetchScalarGridSpec(
            num_scalar_prefetch=1,
            grid=(pairs,),
            in_specs=[block] * 6 + [table] * 3,
            out_specs=[block] * 3 + [pl.BlockSpec((8, wide), lambda h, place: (0, h))],
            scratch_shapes=[pltpu.VMEM((tokens, wide), F32)] * 3,
        ),
        out_shape=[shape] * 3 + [jax.ShapeDtypeStruct((8, heads * HEAD_DIM), F32)],
        compiler_params=pltpu.CompilerParams(vmem_limit_bytes=48 * 2**20),
        cost_estimate=pl.CostEstimate(
            flops=20 * tokens * tokens * wide * pairs, bytes_accessed=30 * tokens * wide * pairs,
            transcendentals=tokens * tokens * heads,
        ),
    )(place, query, keys, values, total, out, grad, *tables)


def causal_blocks(assignment):
    count = assignment.shape[0]
    number = jnp.arange(count, dtype=jnp.int32)
    return jnp.sum(jnp.where(assignment[None, :] == number[:, None], number[None, :], 0), axis=1)


def group_positions(positions, assignment, context, group):
    if group == SEQ_LEN:
        blocks_here = positions.shape[0] // BLK
        start = positions[0] - lax.dynamic_index_in_dim(
            assignment, context * blocks_here, 0, keepdims=False
        ) * BLK
        index = assignment[:, None] * BLK + jnp.arange(BLK, dtype=jnp.int32)[None, :]
        return start + index.reshape(group)
    return lax.all_gather(positions, "context", axis=0, tiled=True)


def rotary_tables(positions):
    half = ROT // 2
    lane = jnp.arange(2 * HEAD_DIM) % HEAD_DIM
    exponent = (lane % half).astype(F32)
    frequency = jnp.where(lane < ROT, 10000.0 ** (-2.0 * exponent / ROT), 0.0)
    angles = positions.astype(F32)[:, None] * frequency[None, :]
    cosine, sine = jnp.cos(angles), jnp.sin(angles)
    low = jnp.where(lane[None, :] < half, -sine, 0.0)
    high = jnp.where((lane[None, :] >= half) & (lane[None, :] < ROT), sine, 0.0)
    return cosine, low, high


def gelu_tanh(value):
    return jax.nn.gelu(value, approximate=True)


def gather_shard(x):
    return lax.all_gather(x, "shard", axis=0, tiled=True)


def scatter_shard(x):
    return lax.psum_scatter(x, "shard", scatter_dimension=0, tiled=True)


def gather_context(x):
    return lax.all_gather(x, "context", axis=0, tiled=True)


def scatter_context(x):
    return lax.psum_scatter(x, "context", scatter_dimension=0, tiled=True)


def local(
    block_input,
    input_weight,
    input_bias,
    output_weight,
    output_bias,
    norm_gain,
    norm_bias,
    assignment,
    positions,
    cotangent,
):
    tokens_here = block_input.shape[0]
    context_size = lax.axis_size("context")
    shard_size = lax.axis_size("shard")
    context = lax.axis_index("context")
    shard_here = lax.axis_index("shard")
    group = tokens_here * context_size
    heads = HEADS // context_size
    attn = heads * HEAD_DIM
    rows_here = input_weight.shape[0]
    inner, segments = column_plan(shard_size, context_size)
    attn_segments = [(base, width) for base, width in segments if base < D]
    hidden_segments = [(base, width) for base, width in segments if base >= D]
    qkv_columns = [(base + i * D, width) for i in range(3) for base, width in attn_segments]
    hidden_columns = [(base + 2 * D, width) for base, width in hidden_segments]

    small = jnp.concatenate(
        [input_bias, output_bias[0], output_bias[1], norm_gain, norm_bias], 0
    ).reshape(1, -1)
    small = gather_shard(small).astype(F32)
    cut = input_bias.shape[0]
    share = norm_gain.shape[0]
    bias_in = small[:, :cut].reshape(-1)
    bias_sum = (small[:, cut : cut + share] + small[:, cut + share : cut + 2 * share]).reshape(-1)
    gain = small[:, cut + 2 * share : cut + 3 * share].reshape(-1)
    shift = small[:, cut + 3 * share :].reshape(-1)

    weight_qkv = gather_shard(take(input_weight, qkv_columns, context, 1))
    weight_hidden = gather_shard(take(input_weight, hidden_columns, context, 1))
    if inner is not None:
        weight_out = gather_shard(take(output_weight, inner, context, 0))
    else:
        weight_out = take(gather_shard(output_weight), segments, context, 0)
    bias_qkv = take(bias_in, qkv_columns, context, 0)
    bias_hidden = take(bias_in, hidden_columns, context, 0)

    centred = block_input - jnp.mean(block_input, axis=1, keepdims=True)
    inverse_std = lax.rsqrt(jnp.mean(centred * centred, axis=1, keepdims=True) + epsilon)
    normalized = centred * inverse_std
    normed = gather_context((normalized * gain + shift).astype(BF16))
    upstream = gather_context(cotangent.astype(BF16))

    place = causal_blocks(assignment)
    tables = rotary_tables(group_positions(positions, assignment, context, group))

    projected = dot(normed, weight_qkv) + bias_qkv
    attended, log_total, query, keys, values = attend(place, projected, tables, heads)
    hidden_pre = dot(normed, weight_hidden) + bias_hidden
    activation = gelu_tanh(hidden_pre).astype(BF16)
    joined = jnp.concatenate([attended, activation], axis=1)
    partial_out = scatter_context(dot(joined, weight_out).astype(BF16))
    block_output = block_input + partial_out.astype(F32) + bias_sum

    attended_grad = dot(upstream, weight_out[:attn], ((1,), (1,))).astype(BF16)
    joined_grad = dot(upstream, weight_out[attn:], ((1,), (1,)))
    hidden_grad = jax.vjp(gelu_tanh, hidden_pre)[1](joined_grad)[0]
    hidden_rounded = hidden_grad.astype(BF16)
    hidden_sum = jnp.sum(hidden_grad, axis=0)
    dq, dk, dv, sums = attend_back(
        place, query, keys, values, log_total, attended, attended_grad, tables, heads
    )
    qkv_rounded = jnp.concatenate([dq, dk, dv], axis=1)
    normed_grad = dot(hidden_rounded, weight_hidden, ((1,), (1,))) + dot(
        qkv_rounded, weight_qkv, ((1,), (1,))
    )
    normed_grad = scatter_context(normed_grad.astype(BF16)).astype(F32)

    out_grad = dot(joined, upstream, ((0,), (0,))).astype(BF16)
    hidden_in_grad = scatter_shard(dot(normed, hidden_rounded, ((0,), (0,))).astype(BF16))
    qkv_in_grad = scatter_shard(dot(normed, qkv_rounded, ((0,), (0,))).astype(BF16))
    if inner is not None:
        out_grad = scatter_shard(out_grad)
        out_grad = gather_context(out_grad[None])
        weight_out_grad = untake(out_grad, inner, 0).astype(F32)
    else:
        whole = jnp.zeros((D + FF, D), BF16)
        at = 0
        for base, width in segments:
            whole = lax.dynamic_update_slice_in_dim(
                whole, out_grad[at : at + width], base + context * width, 0
            )
            at += width
        weight_out_grad = lax.psum(scatter_shard(whole), "context").astype(F32)
    hidden_in_grad = untake(gather_context(hidden_in_grad[None]), hidden_segments, 1)
    qkv_in_grad = gather_context(qkv_in_grad[None])
    qkv_in_grad = untake(qkv_in_grad, qkv_columns, 1)
    weight_in_grad = jnp.concatenate([qkv_in_grad, hidden_in_grad], 1).astype(F32)

    vectors = jnp.concatenate(
        [
            sums[0],
            sums[1],
            sums[2],
            hidden_sum,
            jnp.sum(cotangent, axis=0),
            jnp.sum(normed_grad * normalized, axis=0),
            jnp.sum(normed_grad, axis=0),
        ]
    )
    vectors = jnp.sum(gather_shard(vectors[None]), axis=0)
    vectors = gather_context(vectors[None])
    columns = 3 * attn + hidden_sum.shape[0]
    bias_in_sum = untake(vectors[:, :columns], qkv_columns + hidden_columns, 0)
    others = jnp.sum(vectors[:, columns:], axis=0)

    def own_share(vector):
        length = vector.shape[0] // shard_size
        return lax.dynamic_slice_in_dim(vector, shard_here * length, length, 0)

    bias_row = own_share(others[:D])
    scaled = normed_grad * gain
    input_grad = cotangent + inverse_std * (
        scaled
        - jnp.mean(scaled, axis=1, keepdims=True)
        - normalized * jnp.mean(scaled * normalized, axis=1, keepdims=True)
    )
    return (
        block_output,
        input_grad,
        weight_in_grad,
        own_share(bias_in_sum),
        weight_out_grad,
        jnp.stack([bias_row, bias_row]),
        own_share(others[D : 2 * D]),
        own_share(others[2 * D :]),
    )


def solution(mesh):
    return jax.shard_map(
        local,
        mesh=mesh,
        in_specs=(
            P(("shard", "context"), None),
            P("shard", None),
            P("shard"),
            P("shard", None),
            P(None, "shard"),
            P("shard"),
            P("shard"),
            P(),
            P(("shard", "context")),
            P(("shard", "context"), None),
        ),
        out_specs=(
            P(("shard", "context"), None),
            P(("shard", "context"), None),
            P("shard", None),
            P("shard"),
            P("shard", None),
            P(None, "shard"),
            P("shard"),
            P("shard"),
        ),
        check_vma=False,
    )
```

```python
import functools

import jax
import jax.numpy as jnp
from jax import lax
from jax.experimental import pallas as pl
from jax.experimental.pallas import tpu as pltpu
from jax.sharding import PartitionSpec as P

D = 2048
FF = 8192
HEADS = 32
HEAD_DIM = 64
ROT = 32
SEQ_LEN = 1024
BLK = 128
TILE = 256

epsilon = 1e-05
floor_score = -1e30

F32 = jnp.float32
BF16 = jnp.bfloat16


def dot(a, b, dims=((1,), (0,))):
    return lax.dot_general(a, b, (dims, ((), ())), preferred_element_type=F32)


def column_plan(shard_size, context_size):
    rows = (D + FF) // shard_size
    blocks = rows // HEAD_DIM
    split = HEADS % blocks
    if rows % HEAD_DIM == 0 and split % context_size == 0 and (blocks - split) % context_size == 0:
        inner = [
            (at * HEAD_DIM, size * HEAD_DIM // context_size)
            for at, size in ((0, split), (split, blocks - split))
            if size
        ]
        segments = [(s * rows + at, width) for s in range(shard_size) for at, width in inner]
        return inner, segments
    return None, [(0, D // context_size), (D, FF // context_size)]


def take(array, segments, context, axis):
    parts = [
        lax.dynamic_slice_in_dim(array, base + context * width, width, axis)
        for base, width in segments
    ]
    return jnp.concatenate(parts, axis) if len(parts) > 1 else parts[0]


def untake(gathered, segments, axis):
    parts = []
    at = 0
    for _, width in segments:
        for c in range(gathered.shape[0]):
            parts.append(lax.slice_in_dim(gathered[c], at, at + width, axis=axis))
        at += width
    return jnp.concatenate(parts, axis)


def lane_mask(shape, head):
    lane = lax.broadcasted_iota(jnp.int32, shape, len(shape) - 1)
    return (lane // HEAD_DIM) == head


def rotated(x, cosine, sine_low, sine_high):
    half = ROT // 2
    width = x.shape[1]
    return (
        x * cosine
        + pltpu.roll(x, width - half, 1) * sine_low
        + pltpu.roll(x, half, 1) * sine_high
    )


def stored(place_ref, p):
    return pl.ds(pl.multiple_of(place_ref[p] * BLK, BLK), BLK)


def attend_kernel(
    place_ref, q_ref, k_ref, v_ref, cos_ref, low_ref, high_ref,
    out_ref, total_ref, qr_ref, kr_ref, vr_ref,
):
    tokens = q_ref.shape[0]
    for p in range(tokens // BLK):
        here = pl.ds(p * BLK, BLK)
        there = stored(place_ref, p)
        cosine, low, high = cos_ref[there, :], low_ref[there, :], high_ref[there, :]
        query = rotated(q_ref[there, :], cosine, low, high).astype(BF16)
        qr_ref[here, :] = (query.astype(F32) * HEAD_DIM**-0.5).astype(BF16)
        kr_ref[here, :] = rotated(k_ref[there, :], cosine, low, high).astype(BF16)
        vr_ref[here, :] = v_ref[there, :].astype(BF16)
    for tile in range(tokens // TILE):
        first = tile * TILE // SEQ_LEN * SEQ_LEN
        last = (tile + 1) * TILE
        count = last - first
        query = qr_ref[pl.ds(tile * TILE, TILE), :]
        keys = kr_ref[pl.ds(first, count), :]
        values = vr_ref[pl.ds(first, count), :]
        row = lax.broadcasted_iota(jnp.int32, (TILE, count), 0) + (tile * TILE - first)
        allowed = lax.broadcasted_iota(jnp.int32, (TILE, count), 1) <= row
        outs, totals = [], []
        for head in range(2):
            mine = jnp.where(lane_mask(query.shape, head), query, jnp.zeros_like(query))
            scores = jnp.where(allowed, dot(mine, keys, ((1,), (1,))), floor_score)
            highest = jnp.max(scores, axis=1, keepdims=True)
            weights = jnp.exp(scores - highest)
            total = jnp.sum(weights, axis=1, keepdims=True)
            outs.append(dot(weights.astype(BF16), values) / total)
            totals.append(highest + jnp.log(total))
        wide = (TILE, 2 * HEAD_DIM)
        first_head = lane_mask(wide, 0)
        out = jnp.where(first_head, outs[0], outs[1]).astype(BF16)
        total_ref[pl.ds(tile * TILE, TILE), :] = jnp.where(
            first_head, jnp.broadcast_to(totals[0], wide), jnp.broadcast_to(totals[1], wide)
        )
        for part in range(TILE // BLK):
            out_ref[stored(place_ref, tile * (TILE // BLK) + part), :] = out[
                part * BLK : (part + 1) * BLK
            ]


def attend_back_kernel(
    place_ref, q_ref, k_ref, v_ref, total_ref, out_ref, grad_ref, cos_ref, low_ref, high_ref,
    dq_ref, dk_ref, dv_ref, sums_ref, dq_acc, dk_acc, dv_acc,
):
    tokens = q_ref.shape[0]
    blocks = TILE // BLK
    dk_acc[...] = jnp.zeros_like(dk_acc)
    dv_acc[...] = jnp.zeros_like(dv_acc)
    for tile in range(tokens // TILE):
        first = tile * TILE // SEQ_LEN * SEQ_LEN
        last = (tile + 1) * TILE
        count = last - first
        places = [stored(place_ref, tile * blocks + part) for part in range(blocks)]
        query = q_ref[pl.ds(tile * TILE, TILE), :]
        keys = k_ref[pl.ds(first, count), :]
        values = v_ref[pl.ds(first, count), :]
        grad = jnp.concatenate([grad_ref[place, :] for place in places], 0)
        out = jnp.concatenate([out_ref[place, :] for place in places], 0)
        product = grad.astype(F32) * out.astype(F32)
        row = lax.broadcasted_iota(jnp.int32, (TILE, count), 0) + (tile * TILE - first)
        allowed = lax.broadcasted_iota(jnp.int32, (TILE, count), 1) <= row
        dq = jnp.zeros((TILE, 2 * HEAD_DIM), F32)
        for head in range(2):
            narrow = lane_mask(query.shape, head)
            mine = jnp.where(narrow, query, jnp.zeros_like(query))
            grad_mine = jnp.where(narrow, grad, jnp.zeros_like(grad))
            delta = jnp.sum(jnp.where(narrow, product, 0.0), axis=1, keepdims=True)
            total = total_ref[pl.ds(tile * TILE, TILE), pl.ds(head * HEAD_DIM, 1)]
            scores = jnp.where(allowed, dot(mine, keys, ((1,), (1,))), floor_score)
            weights = jnp.exp(scores - total)
            slope = dot(grad_mine, values, ((1,), (1,)))
            score_grad = (weights * (slope - delta)).astype(BF16)
            rounded = weights.astype(BF16)
            keys_mine = jnp.where(
                lane_mask(keys.shape, head), keys, jnp.zeros_like(keys)
            )
            dq = dq + dot(score_grad, keys_mine)
            dk_acc[pl.ds(first, count), :] += dot(score_grad, mine, ((0,), (0,)))
            dv_acc[pl.ds(first, count), :] += dot(rounded, grad_mine, ((0,), (0,)))
        dq_acc[pl.ds(tile * TILE, TILE), :] = dq * HEAD_DIM**-0.5
    sums = [jnp.zeros((1, 2 * HEAD_DIM), F32) for _ in range(3)]
    for p in range(tokens // BLK):
        here = pl.ds(p * BLK, BLK)
        there = stored(place_ref, p)
        cosine, low, high = cos_ref[there, :], -low_ref[there, :], -high_ref[there, :]
        for i, (acc, ref) in enumerate(((dq_acc, dq_ref), (dk_acc, dk_ref), (dv_acc, dv_ref))):
            part = acc[here, :]
            if i < 2:
                part = rotated(part, cosine, low, high)
            sums[i] = sums[i] + jnp.sum(part, axis=0, keepdims=True)
            ref[there, :] = part.astype(BF16)
    zero = jnp.zeros((5, 2 * HEAD_DIM), F32)
    sums_ref[...] = jnp.concatenate(sums + [zero], 0)


def attend(place, projected, tables, heads):
    tokens = projected.shape[0]
    pairs = heads // 2
    wide = 2 * HEAD_DIM

    def block(offset):
        return pl.BlockSpec((tokens, wide), lambda h, place: (0, h + offset))

    table = pl.BlockSpec((tokens, wide), lambda h, place: (0, 0))
    shape = (tokens, heads * HEAD_DIM)
    return pl.pallas_call(
        attend_kernel,
        grid_spec=pltpu.PrefetchScalarGridSpec(
            num_scalar_prefetch=1,
            grid=(pairs,),
            in_specs=[block(0), block(pairs), block(2 * pairs), table, table, table],
            out_specs=[block(0)] * 5,
        ),
        out_shape=[
            jax.ShapeDtypeStruct(shape, BF16),
            jax.ShapeDtypeStruct(shape, F32),
            jax.ShapeDtypeStruct(shape, BF16),
            jax.ShapeDtypeStruct(shape, BF16),
            jax.ShapeDtypeStruct(shape, BF16),
        ],
        compiler_params=pltpu.CompilerParams(vmem_limit_bytes=48 * 2**20),
        cost_estimate=pl.CostEstimate(
            flops=8 * tokens * tokens * wide * pairs, bytes_accessed=30 * tokens * wide * pairs,
            transcendentals=tokens * tokens * heads,
        ),
    )(place, projected, projected, projected, *tables)


def attend_back(place, query, keys, values, total, out, grad, tables, heads):
    tokens = query.shape[0]
    pairs = heads // 2
    wide = 2 * HEAD_DIM
    block = pl.BlockSpec((tokens, wide), lambda h, place: (0, h))
    table = pl.BlockSpec((tokens, wide), lambda h, place: (0, 0))
    shape = jax.ShapeDtypeStruct((tokens, heads * HEAD_DIM), BF16)
    return pl.pallas_call(
        attend_back_kernel,
        grid_spec=pltpu.PrefetchScalarGridSpec(
            num_scalar_prefetch=1,
            grid=(pairs,),
            in_specs=[block] * 6 + [table] * 3,
            out_specs=[block] * 3 + [pl.BlockSpec((8, wide), lambda h, place: (0, h))],
            scratch_shapes=[pltpu.VMEM((tokens, wide), F32)] * 3,
        ),
        out_shape=[shape] * 3 + [jax.ShapeDtypeStruct((8, heads * HEAD_DIM), F32)],
        compiler_params=pltpu.CompilerParams(vmem_limit_bytes=48 * 2**20),
        cost_estimate=pl.CostEstimate(
            flops=20 * tokens * tokens * wide * pairs, bytes_accessed=30 * tokens * wide * pairs,
            transcendentals=tokens * tokens * heads,
        ),
    )(place, query, keys, values, total, out, grad, *tables)


def causal_blocks(assignment):
    count = assignment.shape[0]
    number = jnp.arange(count, dtype=jnp.int32)
    return jnp.sum(jnp.where(assignment[None, :] == number[:, None], number[None, :], 0), axis=1)


def group_positions(positions, assignment, context, group):
    if group == SEQ_LEN:
        blocks_here = positions.shape[0] // BLK
        start = positions[0] - lax.dynamic_index_in_dim(
            assignment, context * blocks_here, 0, keepdims=False
        ) * BLK
        index = assignment[:, None] * BLK + jnp.arange(BLK, dtype=jnp.int32)[None, :]
        return start + index.reshape(group)
    return lax.all_gather(positions, "context", axis=0, tiled=True)


def rotary_tables(positions):
    half = ROT // 2
    lane = jnp.arange(2 * HEAD_DIM) % HEAD_DIM
    exponent = (lane % half).astype(F32)
    frequency = jnp.where(lane < ROT, 10000.0 ** (-2.0 * exponent / ROT), 0.0)
    angles = positions.astype(F32)[:, None] * frequency[None, :]
    cosine, sine = jnp.cos(angles), jnp.sin(angles)
    low = jnp.where(lane[None, :] < half, -sine, 0.0)
    high = jnp.where((lane[None, :] >= half) & (lane[None, :] < ROT), sine, 0.0)
    return cosine, low, high


def gelu_tanh(value):
    return jax.nn.gelu(value, approximate=True)


def gather_shard(x):
    return lax.all_gather(x, "shard", axis=0, tiled=True)


def scatter_shard(x):
    return lax.psum_scatter(x, "shard", scatter_dimension=0, tiled=True)


def gather_context(x):
    n = lax.axis_size("context")
    context = lax.axis_index("context")
    right = left = x
    before, after = [], []
    for t in range(1, n):
        right = lax.ppermute(right, "context", [(a, a + 1) for a in range(t - 1, n - 1)])
        left = lax.ppermute(left, "context", [(a, a - 1) for a in range(n - t, 0, -1)])
        before.append(right)
        after.append(left)
    rows = x.shape[0]
    line = jnp.concatenate(before[::-1] + [x] + after, 0)
    return lax.dynamic_slice_in_dim(line, (n - 1 - context) * rows, n * rows, 0)


def scatter_context(x):
    n = lax.axis_size("context")
    context = lax.axis_index("context")
    rows = x.shape[0] // n

    def block(j):
        start = jnp.clip(j, 0, n - 1) * rows
        return lax.dynamic_slice_in_dim(x, start, rows, 0)

    def add(mine, received):
        return (mine.astype(F32) + received.astype(F32)).astype(BF16)

    right = left = None
    for t in range(1, n):
        to_right, to_left = block(n - t + context), block(context - (n - t))
        if t > 1:
            to_right, to_left = add(to_right, right), add(to_left, left)
        right = lax.ppermute(to_right, "context", [(a, a + 1) for a in range(t)])
        left = lax.ppermute(to_left, "context", [(n - 1 - a, n - 2 - a) for a in range(t)])
    return block(context).astype(F32) + right.astype(F32) + left.astype(F32)


def local(
    block_input,
    input_weight,
    input_bias,
    output_weight,
    output_bias,
    norm_gain,
    norm_bias,
    assignment,
    positions,
    cotangent,
):
    tokens_here = block_input.shape[0]
    context_size = lax.axis_size("context")
    shard_size = lax.axis_size("shard")
    context = lax.axis_index("context")
    shard_here = lax.axis_index("shard")
    group = tokens_here * context_size
    heads = HEADS // context_size
    attn = heads * HEAD_DIM
    rows_here = input_weight.shape[0]
    inner, segments = column_plan(shard_size, context_size)
    attn_segments = [(base, width) for base, width in segments if base < D]
    hidden_segments = [(base, width) for base, width in segments if base >= D]
    qkv_columns = [(base + i * D, width) for i in range(3) for base, width in attn_segments]
    hidden_columns = [(base + 2 * D, width) for base, width in hidden_segments]

    small = jnp.concatenate(
        [input_bias, output_bias[0], output_bias[1], norm_gain, norm_bias], 0
    ).reshape(1, -1)
    small = gather_shard(small).astype(F32)
    cut = input_bias.shape[0]
    share = norm_gain.shape[0]
    bias_in = small[:, :cut].reshape(-1)
    bias_sum = (small[:, cut : cut + share] + small[:, cut + share : cut + 2 * share]).reshape(-1)
    gain = small[:, cut + 2 * share : cut + 3 * share].reshape(-1)
    shift = small[:, cut + 3 * share :].reshape(-1)

    weight_qkv = gather_shard(take(input_weight, qkv_columns, context, 1))
    weight_hidden = gather_shard(take(input_weight, hidden_columns, context, 1))
    if inner is not None:
        weight_out = gather_shard(take(output_weight, inner, context, 0))
    else:
        weight_out = take(gather_shard(output_weight), segments, context, 0)
    bias_qkv = take(bias_in, qkv_columns, context, 0)
    bias_hidden = take(bias_in, hidden_columns, context, 0)

    centred = block_input - jnp.mean(block_input, axis=1, keepdims=True)
    inverse_std = lax.rsqrt(jnp.mean(centred * centred, axis=1, keepdims=True) + epsilon)
    normalized = centred * inverse_std
    normed = gather_context((normalized * gain + shift).astype(BF16))
    upstream = gather_context(cotangent.astype(BF16))

    place = causal_blocks(assignment)
    tables = rotary_tables(group_positions(positions, assignment, context, group))

    projected = dot(normed, weight_qkv) + bias_qkv
    attended, log_total, query, keys, values = attend(place, projected, tables, heads)
    hidden_pre = dot(normed, weight_hidden) + bias_hidden
    activation = gelu_tanh(hidden_pre).astype(BF16)
    joined = jnp.concatenate([attended, activation], axis=1)
    partial_out = scatter_context(dot(joined, weight_out).astype(BF16))
    block_output = block_input + partial_out + bias_sum

    attended_grad = dot(upstream, weight_out[:attn], ((1,), (1,))).astype(BF16)
    joined_grad = dot(upstream, weight_out[attn:], ((1,), (1,)))
    hidden_grad = jax.vjp(gelu_tanh, hidden_pre)[1](joined_grad)[0]
    hidden_rounded = hidden_grad.astype(BF16)
    hidden_sum = jnp.sum(hidden_grad, axis=0)
    dq, dk, dv, sums = attend_back(
        place, query, keys, values, log_total, attended, attended_grad, tables, heads
    )
    qkv_rounded = jnp.concatenate([dq, dk, dv], axis=1)
    normed_grad = dot(hidden_rounded, weight_hidden, ((1,), (1,))) + dot(
        qkv_rounded, weight_qkv, ((1,), (1,))
    )
    normed_grad = scatter_context(normed_grad.astype(BF16))

    out_grad = dot(joined, upstream, ((0,), (0,))).astype(BF16)
    hidden_in_grad = scatter_shard(dot(normed, hidden_rounded, ((0,), (0,))).astype(BF16))
    qkv_in_grad = scatter_shard(dot(normed, qkv_rounded, ((0,), (0,))).astype(BF16))
    if inner is not None:
        out_grad = scatter_shard(out_grad)
        out_grad = gather_context(out_grad[None])
        weight_out_grad = untake(out_grad, inner, 0).astype(F32)
    else:
        whole = jnp.zeros((D + FF, D), BF16)
        at = 0
        for base, width in segments:
            whole = lax.dynamic_update_slice_in_dim(
                whole, out_grad[at : at + width], base + context * width, 0
            )
            at += width
        weight_out_grad = lax.psum(scatter_shard(whole), "context").astype(F32)
    hidden_in_grad = untake(gather_context(hidden_in_grad[None]), hidden_segments, 1)
    qkv_in_grad = gather_context(qkv_in_grad[None])
    qkv_in_grad = untake(qkv_in_grad, qkv_columns, 1)
    weight_in_grad = jnp.concatenate([qkv_in_grad, hidden_in_grad], 1).astype(F32)

    vectors = jnp.concatenate(
        [
            sums[0],
            sums[1],
            sums[2],
            hidden_sum,
            jnp.sum(cotangent, axis=0),
            jnp.sum(normed_grad * normalized, axis=0),
            jnp.sum(normed_grad, axis=0),
        ]
    )
    vectors = jnp.sum(gather_shard(vectors[None]), axis=0)
    vectors = lax.all_gather(vectors, "context")
    columns = 3 * attn + hidden_sum.shape[0]
    bias_in_sum = untake(vectors[:, :columns], qkv_columns + hidden_columns, 0)
    others = jnp.sum(vectors[:, columns:], axis=0)

    def own_share(vector):
        length = vector.shape[0] // shard_size
        return lax.dynamic_slice_in_dim(vector, shard_here * length, length, 0)

    bias_row = own_share(others[:D])
    scaled = normed_grad * gain
    input_grad = cotangent + inverse_std * (
        scaled
        - jnp.mean(scaled, axis=1, keepdims=True)
        - normalized * jnp.mean(scaled * normalized, axis=1, keepdims=True)
    )
    return (
        block_output,
        input_grad,
        weight_in_grad,
        own_share(bias_in_sum),
        weight_out_grad,
        jnp.stack([bias_row, bias_row]),
        own_share(others[D : 2 * D]),
        own_share(others[2 * D :]),
    )


def solution(mesh):
    return jax.shard_map(
        local,
        mesh=mesh,
        in_specs=(
            P(("shard", "context"), None),
            P("shard", None),
            P("shard"),
            P("shard", None),
            P(None, "shard"),
            P("shard"),
            P("shard"),
            P(),
            P(("shard", "context")),
            P(("shard", "context"), None),
        ),
        out_specs=(
            P(("shard", "context"), None),
            P(("shard", "context"), None),
            P("shard", None),
            P("shard"),
            P("shard", None),
            P(None, "shard"),
            P("shard"),
            P("shard"),
        ),
        check_vma=False,
    )
```

```python
import functools

import jax
import jax.numpy as jnp
from jax import lax
from jax.experimental import pallas as pl
from jax.experimental.pallas import tpu as pltpu
from jax.sharding import PartitionSpec as P

D = 2048
FF = 8192
HEADS = 32
HEAD_DIM = 64
ROT = 32
SEQ_LEN = 1024
BLK = 128
TILE = 256

epsilon = 1e-05
floor_score = -1e30

F32 = jnp.float32
BF16 = jnp.bfloat16


def dot(a, b, dims=((1,), (0,))):
    return lax.dot_general(a, b, (dims, ((), ())), preferred_element_type=F32)


def column_plan(shard_size, context_size):
    rows = (D + FF) // shard_size
    blocks = rows // HEAD_DIM
    split = HEADS % blocks
    if rows % HEAD_DIM == 0 and split % context_size == 0 and (blocks - split) % context_size == 0:
        inner = [
            (at * HEAD_DIM, size * HEAD_DIM // context_size)
            for at, size in ((0, split), (split, blocks - split))
            if size
        ]
        segments = [(s * rows + at, width) for s in range(shard_size) for at, width in inner]
        return inner, segments
    return None, [(0, D // context_size), (D, FF // context_size)]


def take(array, segments, context, axis):
    parts = [
        lax.dynamic_slice_in_dim(array, base + context * width, width, axis)
        for base, width in segments
    ]
    return jnp.concatenate(parts, axis) if len(parts) > 1 else parts[0]


def untake(gathered, segments, axis):
    parts = []
    at = 0
    for _, width in segments:
        for c in range(gathered.shape[0]):
            parts.append(lax.slice_in_dim(gathered[c], at, at + width, axis=axis))
        at += width
    return jnp.concatenate(parts, axis)


def lane_mask(shape, head):
    lane = lax.broadcasted_iota(jnp.int32, shape, len(shape) - 1)
    return (lane // HEAD_DIM) == head


def rotated(x, cosine, sine_low, sine_high):
    half = ROT // 2
    width = x.shape[1]
    return (
        x * cosine
        + pltpu.roll(x, width - half, 1) * sine_low
        + pltpu.roll(x, half, 1) * sine_high
    )


def stored(place_ref, p):
    return pl.ds(pl.multiple_of(place_ref[p] * BLK, BLK), BLK)


def attend_kernel(
    place_ref, q_ref, k_ref, v_ref, cos_ref, low_ref, high_ref,
    out_ref, total_ref, qr_ref, kr_ref, vr_ref,
):
    tokens = q_ref.shape[0]
    for p in range(tokens // BLK):
        here = pl.ds(p * BLK, BLK)
        there = stored(place_ref, p)
        cosine, low, high = cos_ref[there, :], low_ref[there, :], high_ref[there, :]
        query = rotated(q_ref[there, :], cosine, low, high).astype(BF16)
        qr_ref[here, :] = (query.astype(F32) * HEAD_DIM**-0.5).astype(BF16)
        kr_ref[here, :] = rotated(k_ref[there, :], cosine, low, high).astype(BF16)
        vr_ref[here, :] = v_ref[there, :].astype(BF16)
    for tile in range(tokens // TILE):
        first = tile * TILE // SEQ_LEN * SEQ_LEN
        last = (tile + 1) * TILE
        count = last - first
        query = qr_ref[pl.ds(tile * TILE, TILE), :]
        keys = kr_ref[pl.ds(first, count), :]
        values = vr_ref[pl.ds(first, count), :]
        row = lax.broadcasted_iota(jnp.int32, (TILE, count), 0) + (tile * TILE - first)
        allowed = lax.broadcasted_iota(jnp.int32, (TILE, count), 1) <= row
        outs, totals = [], []
        for head in range(2):
            mine = jnp.where(lane_mask(query.shape, head), query, jnp.zeros_like(query))
            scores = jnp.where(allowed, dot(mine, keys, ((1,), (1,))), floor_score)
            highest = jnp.max(scores, axis=1, keepdims=True)
            weights = jnp.exp(scores - highest)
            total = jnp.sum(weights, axis=1, keepdims=True)
            outs.append(dot(weights.astype(BF16), values) / total)
            totals.append(highest + jnp.log(total))
        wide = (TILE, 2 * HEAD_DIM)
        first_head = lane_mask(wide, 0)
        out = jnp.where(first_head, outs[0], outs[1]).astype(BF16)
        total_ref[pl.ds(tile * TILE, TILE), :] = jnp.where(
            first_head, jnp.broadcast_to(totals[0], wide), jnp.broadcast_to(totals[1], wide)
        )
        for part in range(TILE // BLK):
            out_ref[stored(place_ref, tile * (TILE // BLK) + part), :] = out[
                part * BLK : (part + 1) * BLK
            ]


def attend_back_kernel(
    place_ref, q_ref, k_ref, v_ref, total_ref, out_ref, grad_ref, cos_ref, low_ref, high_ref,
    dq_ref, dk_ref, dv_ref, sums_ref, dq_acc, dk_acc, dv_acc,
):
    tokens = q_ref.shape[0]
    blocks = TILE // BLK
    dk_acc[...] = jnp.zeros_like(dk_acc)
    dv_acc[...] = jnp.zeros_like(dv_acc)
    for tile in range(tokens // TILE):
        first = tile * TILE // SEQ_LEN * SEQ_LEN
        last = (tile + 1) * TILE
        count = last - first
        places = [stored(place_ref, tile * blocks + part) for part in range(blocks)]
        query = q_ref[pl.ds(tile * TILE, TILE), :]
        keys = k_ref[pl.ds(first, count), :]
        values = v_ref[pl.ds(first, count), :]
        grad = jnp.concatenate([grad_ref[place, :] for place in places], 0)
        out = jnp.concatenate([out_ref[place, :] for place in places], 0)
        product = grad.astype(F32) * out.astype(F32)
        row = lax.broadcasted_iota(jnp.int32, (TILE, count), 0) + (tile * TILE - first)
        allowed = lax.broadcasted_iota(jnp.int32, (TILE, count), 1) <= row
        dq = jnp.zeros((TILE, 2 * HEAD_DIM), F32)
        for head in range(2):
            narrow = lane_mask(query.shape, head)
            mine = jnp.where(narrow, query, jnp.zeros_like(query))
            grad_mine = jnp.where(narrow, grad, jnp.zeros_like(grad))
            delta = jnp.sum(jnp.where(narrow, product, 0.0), axis=1, keepdims=True)
            total = total_ref[pl.ds(tile * TILE, TILE), pl.ds(head * HEAD_DIM, 1)]
            scores = jnp.where(allowed, dot(mine, keys, ((1,), (1,))), floor_score)
            weights = jnp.exp(scores - total)
            slope = dot(grad_mine, values, ((1,), (1,)))
            score_grad = (weights * (slope - delta)).astype(BF16)
            rounded = weights.astype(BF16)
            keys_mine = jnp.where(
                lane_mask(keys.shape, head), keys, jnp.zeros_like(keys)
            )
            dq = dq + dot(score_grad, keys_mine)
            dk_acc[pl.ds(first, count), :] += dot(score_grad, mine, ((0,), (0,)))
            dv_acc[pl.ds(first, count), :] += dot(rounded, grad_mine, ((0,), (0,)))
        dq_acc[pl.ds(tile * TILE, TILE), :] = dq * HEAD_DIM**-0.5
    sums = [jnp.zeros((1, 2 * HEAD_DIM), F32) for _ in range(3)]
    for p in range(tokens // BLK):
        here = pl.ds(p * BLK, BLK)
        there = stored(place_ref, p)
        cosine, low, high = cos_ref[there, :], -low_ref[there, :], -high_ref[there, :]
        for i, (acc, ref) in enumerate(((dq_acc, dq_ref), (dk_acc, dk_ref), (dv_acc, dv_ref))):
            part = acc[here, :]
            if i < 2:
                part = rotated(part, cosine, low, high)
            sums[i] = sums[i] + jnp.sum(part, axis=0, keepdims=True)
            ref[there, :] = part.astype(BF16)
    zero = jnp.zeros((5, 2 * HEAD_DIM), F32)
    sums_ref[...] = jnp.concatenate(sums + [zero], 0)


def attend(place, projected, tables, heads):
    tokens = projected.shape[0]
    pairs = heads // 2
    wide = 2 * HEAD_DIM

    def block(offset):
        return pl.BlockSpec((tokens, wide), lambda h, place: (0, h + offset))

    table = pl.BlockSpec((tokens, wide), lambda h, place: (0, 0))
    shape = (tokens, heads * HEAD_DIM)
    return pl.pallas_call(
        attend_kernel,
        grid_spec=pltpu.PrefetchScalarGridSpec(
            num_scalar_prefetch=1,
            grid=(pairs,),
            in_specs=[block(0), block(pairs), block(2 * pairs), table, table, table],
            out_specs=[block(0)] * 5,
        ),
        out_shape=[
            jax.ShapeDtypeStruct(shape, BF16),
            jax.ShapeDtypeStruct(shape, F32),
            jax.ShapeDtypeStruct(shape, BF16),
            jax.ShapeDtypeStruct(shape, BF16),
            jax.ShapeDtypeStruct(shape, BF16),
        ],
        compiler_params=pltpu.CompilerParams(vmem_limit_bytes=48 * 2**20),
        cost_estimate=pl.CostEstimate(
            flops=8 * tokens * tokens * wide * pairs, bytes_accessed=30 * tokens * wide * pairs,
            transcendentals=tokens * tokens * heads,
        ),
    )(place, projected, projected, projected, *tables)


def attend_back(place, query, keys, values, total, out, grad, tables, heads):
    tokens = query.shape[0]
    pairs = heads // 2
    wide = 2 * HEAD_DIM
    block = pl.BlockSpec((tokens, wide), lambda h, place: (0, h))
    table = pl.BlockSpec((tokens, wide), lambda h, place: (0, 0))
    shape = jax.ShapeDtypeStruct((tokens, heads * HEAD_DIM), BF16)
    return pl.pallas_call(
        attend_back_kernel,
        grid_spec=pltpu.PrefetchScalarGridSpec(
            num_scalar_prefetch=1,
            grid=(pairs,),
            in_specs=[block] * 6 + [table] * 3,
            out_specs=[block] * 3 + [pl.BlockSpec((8, wide), lambda h, place: (0, h))],
            scratch_shapes=[pltpu.VMEM((tokens, wide), F32)] * 3,
        ),
        out_shape=[shape] * 3 + [jax.ShapeDtypeStruct((8, heads * HEAD_DIM), F32)],
        compiler_params=pltpu.CompilerParams(vmem_limit_bytes=48 * 2**20),
        cost_estimate=pl.CostEstimate(
            flops=20 * tokens * tokens * wide * pairs, bytes_accessed=30 * tokens * wide * pairs,
            transcendentals=tokens * tokens * heads,
        ),
    )(place, query, keys, values, total, out, grad, *tables)


def causal_blocks(assignment):
    count = assignment.shape[0]
    number = jnp.arange(count, dtype=jnp.int32)
    return jnp.sum(jnp.where(assignment[None, :] == number[:, None], number[None, :], 0), axis=1)


def group_positions(positions, assignment, context, group):
    if group == SEQ_LEN:
        blocks_here = positions.shape[0] // BLK
        start = positions[0] - lax.dynamic_index_in_dim(
            assignment, context * blocks_here, 0, keepdims=False
        ) * BLK
        index = assignment[:, None] * BLK + jnp.arange(BLK, dtype=jnp.int32)[None, :]
        return start + index.reshape(group)
    return lax.all_gather(positions, "context", axis=0, tiled=True)


def rotary_tables(positions):
    half = ROT // 2
    lane = jnp.arange(2 * HEAD_DIM) % HEAD_DIM
    exponent = (lane % half).astype(F32)
    frequency = jnp.where(lane < ROT, 10000.0 ** (-2.0 * exponent / ROT), 0.0)
    angles = positions.astype(F32)[:, None] * frequency[None, :]
    cosine, sine = jnp.cos(angles), jnp.sin(angles)
    low = jnp.where(lane[None, :] < half, -sine, 0.0)
    high = jnp.where((lane[None, :] >= half) & (lane[None, :] < ROT), sine, 0.0)
    return cosine, low, high


def gelu_tanh(value):
    return jax.nn.gelu(value, approximate=True)


def tie(value, *after):
    return lax.optimization_barrier((value, after))[0] if after else value


def close(lines, *values):
    arrived, values = lax.optimization_barrier(([line.latest for line in lines], values))
    for line, arrays in zip(lines, arrived):
        line.latest = arrays
    return jax.tree.leaves(arrived) + jax.tree.leaves(values), values


class LineGather:
    def __init__(self, block):
        self.block, self.before, self.after = block, [], []

    def step(self, *after):
        n = lax.axis_size("context")
        t = len(self.before) + 1
        right, left = (self.before[-1], self.after[-1]) if t > 1 else (self.block, self.block)
        right, left = tie((right, left), *after)
        self.before.append(
            lax.ppermute(right, "context", [(a, a + 1) for a in range(t - 1, n - 1)])
        )
        self.after.append(lax.ppermute(left, "context", [(a, a - 1) for a in range(n - t, 0, -1)]))
        return self.before[-1], self.after[-1]

    @property
    def latest(self):
        return self.before[-1], self.after[-1]

    @latest.setter
    def latest(self, arrays):
        self.before[-1], self.after[-1] = arrays

    def whole(self, context):
        return place(context, self.before[::-1] + [self.block] + self.after)


class LineScatter:
    def __init__(self, partial):
        self.partial, self.steps = partial, 0
        self.right = self.left = None

    def mine(self, j):
        n = lax.axis_size("context")
        rows = self.partial.shape[0] // n
        return lax.dynamic_slice_in_dim(self.partial, jnp.clip(j, 0, n - 1) * rows, rows, 0)

    def step(self, *after):
        n = lax.axis_size("context")
        context = lax.axis_index("context")
        self.steps = t = self.steps + 1
        right, left = self.mine(n - t + context), self.mine(context - (n - t))
        if t > 1:
            right = (right.astype(F32) + self.right.astype(F32)).astype(BF16)
            left = (left.astype(F32) + self.left.astype(F32)).astype(BF16)
        right, left = tie((right, left), *after)
        self.right = lax.ppermute(right, "context", [(a, a + 1) for a in range(t)])
        self.left = lax.ppermute(left, "context", [(n - 1 - a, n - 2 - a) for a in range(t)])
        return self.right, self.left

    @property
    def latest(self):
        return self.right, self.left

    @latest.setter
    def latest(self, arrays):
        self.right, self.left = arrays

    def result(self):
        own = self.mine(lax.axis_index("context")).astype(F32)
        return own + self.right.astype(F32) + self.left.astype(F32)


def place_kernel(context_ref, *refs):
    *blocks, out_ref, held, taken, given = refs
    n = (len(blocks) + 1) // 2
    rows = blocks[0].shape[0]

    def give(j):
        return pltpu.make_async_copy(
            held.at[j], out_ref.at[pl.ds(j * rows, rows), :], given.at[j]
        )

    for c in range(n):

        @pl.when(context_ref[0] == c)
        def _():
            copies = [
                pltpu.make_async_copy(blocks[j - c + n - 1], held.at[j], taken.at[j])
                for j in range(n)
            ]
            for copy in copies:
                copy.start()
            for j, copy in enumerate(copies):
                copy.wait()
                give(j).start()
            for j in range(n):
                give(j).wait()


def place(context, line):
    n = (len(line) + 1) // 2
    rows, columns = line[0].shape
    anywhere = pl.BlockSpec(memory_space=pl.ANY)
    return pl.pallas_call(
        place_kernel,
        grid_spec=pltpu.PrefetchScalarGridSpec(
            num_scalar_prefetch=1,
            grid=(1,),
            in_specs=[anywhere] * len(line),
            out_specs=anywhere,
            scratch_shapes=[
                pltpu.VMEM((n, rows, columns), line[0].dtype),
                pltpu.SemaphoreType.DMA((n,)),
                pltpu.SemaphoreType.DMA((n,)),
            ],
        ),
        out_shape=jax.ShapeDtypeStruct((n * rows, columns), line[0].dtype),
        compiler_params=pltpu.CompilerParams(vmem_limit_bytes=32 * 2**20),
        cost_estimate=pl.CostEstimate(
            flops=0, bytes_accessed=4 * n * rows * columns, transcendentals=0
        ),
    )(context.reshape(1), *line)


def gather_shard(x):
    return lax.all_gather(x, "shard", axis=0, tiled=True)


def scatter_shard(x):
    return lax.psum_scatter(x, "shard", scatter_dimension=0, tiled=True)


def spread_kernel(segments, in_ref, *refs):
    out_ref = refs[-1]
    for c in range(in_ref.shape[0]):
        part = in_ref[c].astype(F32)
        at = 0
        for base, width in segments:
            out_ref[:, base + c * width : base + (c + 1) * width] = part[:, at : at + width]
            at += width


def finish_hidden(parts, segments, rows, columns):
    n = parts.shape[0]
    step = 32
    return pl.pallas_call(
        functools.partial(spread_kernel, segments),
        grid=(rows // step,),
        in_specs=[pl.BlockSpec((n, step, parts.shape[2]), lambda i: (0, i, 0))],
        out_specs=pl.BlockSpec((step, columns), lambda i: (i, 0)),
        out_shape=jax.ShapeDtypeStruct((rows, columns), F32),
        compiler_params=pltpu.CompilerParams(vmem_limit_bytes=48 * 2**20),
        cost_estimate=pl.CostEstimate(
            flops=0, bytes_accessed=5 * rows * columns, transcendentals=0
        ),
    )(parts)


def finish_qkv(whole, parts, segments):
    n = parts.shape[0]
    rows = whole.shape[0]
    step = 32
    columns = n * sum(width for _, width in segments)
    return pl.pallas_call(
        functools.partial(spread_kernel, segments),
        grid=(rows // step,),
        in_specs=[
            pl.BlockSpec((n, step, parts.shape[2]), lambda i: (0, i, 0)),
            pl.BlockSpec(memory_space=pl.ANY),
        ],
        out_specs=pl.BlockSpec((step, columns), lambda i: (i, 0)),
        out_shape=jax.ShapeDtypeStruct(whole.shape, F32),
        input_output_aliases={1: 0},
        compiler_params=pltpu.CompilerParams(vmem_limit_bytes=48 * 2**20),
        cost_estimate=pl.CostEstimate(
            flops=0, bytes_accessed=6 * rows * columns, transcendentals=0
        ),
    )(parts, whole)


def finish_out_kernel(in_ref, out_ref):
    out_ref[...] = in_ref[0].astype(F32)


def finish_out(gathered, inner):
    n, rows, columns = gathered.shape
    step = HEAD_DIM
    bounds, at = [], 0
    for base, width in inner:
        bounds.append((base // step, width // step, at // step))
        at += width

    def source(b):
        c = first = 0
        for base, width, start in bounds:
            inside = b >= base
            c = jnp.where(inside, (b - base) // width, c)
            first = jnp.where(inside, start + (b - base) % width, first)
        return (c, first, 0)

    return pl.pallas_call(
        finish_out_kernel,
        grid=(n * rows // step,),
        in_specs=[pl.BlockSpec((1, step, columns), source)],
        out_specs=pl.BlockSpec((step, columns), lambda b: (b, 0)),
        out_shape=jax.ShapeDtypeStruct((n * rows, columns), F32),
        cost_estimate=pl.CostEstimate(
            flops=0, bytes_accessed=6 * n * rows * columns, transcendentals=0
        ),
    )(gathered)


def local(
    block_input,
    input_weight,
    input_bias,
    output_weight,
    output_bias,
    norm_gain,
    norm_bias,
    assignment,
    positions,
    cotangent,
):
    tokens_here = block_input.shape[0]
    context_size = lax.axis_size("context")
    shard_size = lax.axis_size("shard")
    context = lax.axis_index("context")
    shard_here = lax.axis_index("shard")
    group = tokens_here * context_size
    heads = HEADS // context_size
    attn = heads * HEAD_DIM
    rows_here = input_weight.shape[0]
    steps = context_size - 1
    inner, segments = column_plan(shard_size, context_size)
    attn_segments = [(base, width) for base, width in segments if base < D]
    hidden_segments = [(base, width) for base, width in segments if base >= D]
    qkv_columns = [(base + i * D, width) for i in range(3) for base, width in attn_segments]
    hidden_columns = [(base + 2 * D, width) for base, width in hidden_segments]

    up = LineGather(cotangent.astype(BF16))
    up.step()

    small = jnp.concatenate(
        [input_bias, output_bias[0], output_bias[1], norm_gain, norm_bias], 0
    ).reshape(1, -1)
    small = gather_shard(small).astype(F32)
    cut = input_bias.shape[0]
    share = norm_gain.shape[0]
    bias_in = small[:, :cut].reshape(-1)
    bias_sum = (small[:, cut : cut + share] + small[:, cut + share : cut + 2 * share]).reshape(-1)
    gain = small[:, cut + 2 * share : cut + 3 * share].reshape(-1)
    shift = small[:, cut + 3 * share :].reshape(-1)

    centred = block_input - jnp.mean(block_input, axis=1, keepdims=True)
    inverse_std = lax.rsqrt(jnp.mean(centred * centred, axis=1, keepdims=True) + epsilon)
    normalized = centred * inverse_std
    normed_here = (normalized * gain + shift).astype(BF16)

    weight_qkv = gather_shard(take(input_weight, qkv_columns, context, 1))
    gate, (normed_here, input_weight, output_weight) = close(
        [up], normed_here, input_weight, output_weight
    )
    weight_hidden = gather_shard(take(input_weight, hidden_columns, context, 1))
    if inner is not None:
        weight_out = gather_shard(take(output_weight, inner, context, 0))
    else:
        weight_out = take(gather_shard(output_weight), segments, context, 0)
    bias_qkv = take(bias_in, qkv_columns, context, 0)
    bias_hidden = take(bias_in, hidden_columns, context, 0)
    places = causal_blocks(assignment)

    norm = LineGather(normed_here)
    for t in range(steps):
        gate = norm.step(*gate)
        if t == 0:
            positions = tie(positions, *gate)
            tables = rotary_tables(group_positions(positions, assignment, context, group))
    normed = norm.whole(context)

    normed = tie(normed, *gate)
    projected = dot(normed, weight_qkv) + bias_qkv
    up.step(*gate)
    attended, log_total, query, keys, values = attend(places, projected, tables, heads)
    gate, (attended, normed) = close([up], attended, normed)
    for t in range(steps - 2):
        up.step(*gate)
    hidden_pre = dot(normed, weight_hidden) + bias_hidden
    activation = gelu_tanh(hidden_pre).astype(BF16)
    joined = jnp.concatenate([attended, activation], axis=1)
    partial_out = dot(joined, weight_out).astype(BF16)
    gate, (partial_out, joined) = close([up], partial_out, joined)
    upstream = up.whole(context)

    out = LineScatter(partial_out)
    out.step()
    out_grad = dot(joined, upstream, ((0,), (0,))).astype(BF16)
    gate, (out_grad, upstream) = close([out], out_grad, upstream)
    if inner is not None:
        out_grad_sum = scatter_shard(out_grad)

    out.step()
    joined_grad = dot(upstream, weight_out[attn:], ((1,), (1,)))
    hidden_grad = jax.vjp(gelu_tanh, hidden_pre)[1](joined_grad)[0]
    hidden_rounded = hidden_grad.astype(BF16)
    hidden_sum = jnp.sum(hidden_grad, axis=0)
    gate, (hidden_rounded, upstream) = close([out], hidden_rounded, upstream)

    for t in range(steps - 2):
        out.step()
    hidden_in_grad = dot(normed, hidden_rounded, ((0,), (0,))).astype(BF16)
    gate, (hidden_in_grad, hidden_rounded, upstream) = close(
        [out], hidden_in_grad, hidden_rounded, upstream
    )
    hidden_in_sum = scatter_shard(hidden_in_grad)
    block_output = block_input + out.result() + bias_sum

    attended_grad = dot(upstream, weight_out[:attn], ((1,), (1,))).astype(BF16)
    normed_grad = dot(hidden_rounded, weight_hidden, ((1,), (1,)))
    attended_grad, normed_grad = lax.optimization_barrier((attended_grad, normed_grad))

    gathers = []
    if inner is not None:
        gathers.append(LineGather(out_grad_sum))
        gathers[0].step(attended_grad)
    dq, dk, dv, sums = attend_back(
        places, query, keys, values, log_total, attended, attended_grad, tables, heads
    )
    qkv_rounded = jnp.concatenate([dq, dk, dv], axis=1)
    gate, (qkv_rounded,) = close(gathers, qkv_rounded)

    for gather in gathers:
        gather.step()
    normed_grad = normed_grad + dot(qkv_rounded, weight_qkv, ((1,), (1,)))
    gain_sum = jnp.sum(normed_grad * ((normed.astype(F32) - shift) / gain), axis=0)
    shift_sum = jnp.sum(normed_grad, axis=0)
    partial_grad = normed_grad.astype(BF16)
    gate, (partial_grad, qkv_rounded) = close(gathers, partial_grad, qkv_rounded)

    grad = LineScatter(partial_grad)
    for gather in gathers:
        for t in range(2, steps):
            gather.step()
    grad.step()
    qkv_in_grad = dot(normed, qkv_rounded, ((0,), (0,))).astype(BF16)
    gate, (qkv_in_grad,) = close(gathers + [grad], qkv_in_grad)
    vectors = jnp.concatenate(
        [sums[0], sums[1], sums[2], hidden_sum, jnp.sum(cotangent, axis=0), gain_sum, shift_sum]
    )
    wide = 3 * attn
    extra = -(-vectors.shape[0] // (16 * wide)) * 16
    vectors = jnp.pad(vectors, (0, extra * wide - vectors.shape[0])).reshape(1, extra, wide)
    vectors = jnp.broadcast_to(vectors.astype(BF16), (shard_size, extra, wide))
    qkv_in_sum = scatter_shard(
        jnp.concatenate([qkv_in_grad.reshape(shard_size, rows_here, wide), vectors], 1).reshape(
            -1, wide
        )
    )

    hidden_gather, qkv_gather = LineGather(hidden_in_sum), LineGather(qkv_in_sum)
    if inner is not None:
        weight_out_grad = finish_out(
            tie(gathers[0].whole(context), *gate).reshape(context_size, -1, D), inner
        )
        done = (weight_out_grad,)
    else:
        done = ()
    for t in range(steps):
        lines = [hidden_gather]
        hidden_gather.step(*gate)
        if t == steps - 1 and grad.steps < steps:
            grad.step()
            lines.append(grad)
        gate, done = close(lines, *done)
        if inner is not None and t == 0:
            (weight_out_grad,) = done
            done = ()
    hidden_parts = hidden_gather.whole(context).reshape(context_size, rows_here, -1)
    weight_in_grad = finish_hidden(
        tie(hidden_parts, *gate), hidden_columns, rows_here, input_weight.shape[1]
    )
    for t in range(steps):
        lines = [qkv_gather]
        qkv_gather.step(*gate)
        if grad.steps < steps:
            grad.step()
            lines.append(grad)
        gate, done = close(lines, *((weight_in_grad,) if t == 0 else ()))
        if t == 0:
            (weight_in_grad,) = done
    if inner is None:
        whole = jnp.zeros((D + FF, D), BF16)
        at = 0
        for base, width in segments:
            whole = lax.dynamic_update_slice_in_dim(
                whole, out_grad[at : at + width], base + context * width, 0
            )
            at += width
        weight_out_grad = lax.psum(scatter_shard(whole), "context").astype(F32)
    qkv_parts = qkv_gather.whole(context).reshape(context_size, rows_here + extra, wide)
    weight_in_grad = finish_qkv(weight_in_grad, qkv_parts, qkv_columns)

    vectors = qkv_parts[:, rows_here:].astype(F32).reshape(context_size, -1)
    columns = wide + hidden_sum.shape[0]
    bias_in_sum = untake(vectors[:, :columns], qkv_columns + hidden_columns, 0)
    others = jnp.sum(vectors[:, columns : columns + 3 * D], axis=0)

    def own_share(vector):
        length = vector.shape[0] // shard_size
        return lax.dynamic_slice_in_dim(vector, shard_here * length, length, 0)

    bias_row = own_share(others[:D])
    normed_grad = grad.result()
    scaled = normed_grad * gain
    input_grad = cotangent + inverse_std * (
        scaled
        - jnp.mean(scaled, axis=1, keepdims=True)
        - normalized * jnp.mean(scaled * normalized, axis=1, keepdims=True)
    )
    return (
        block_output,
        input_grad,
        weight_in_grad,
        own_share(bias_in_sum),
        weight_out_grad,
        jnp.stack([bias_row, bias_row]),
        own_share(others[D : 2 * D]),
        own_share(others[2 * D :]),
    )


def solution(mesh):
    return jax.shard_map(
        local,
        mesh=mesh,
        in_specs=(
            P(("shard", "context"), None),
            P("shard", None),
            P("shard"),
            P("shard", None),
            P(None, "shard"),
            P("shard"),
            P("shard"),
            P(),
            P(("shard", "context")),
            P(("shard", "context"), None),
        ),
        out_specs=(
            P(("shard", "context"), None),
            P(("shard", "context"), None),
            P("shard", None),
            P("shard"),
            P("shard", None),
            P(None, "shard"),
            P("shard"),
            P("shard"),
        ),
        check_vma=False,
    )
```

```python
import functools

import jax
import jax.numpy as jnp
from jax import lax
from jax.experimental import pallas as pl
from jax.experimental.pallas import tpu as pltpu
from jax.sharding import PartitionSpec as P

D = 2048
FF = 8192
HEADS = 32
HEAD_DIM = 64
ROT = 32
SEQ_LEN = 1024
BLK = 128
TILE = 256

epsilon = 1e-05
floor_score = -1e30

F32 = jnp.float32
BF16 = jnp.bfloat16


def dot(a, b, dims=((1,), (0,))):
    return lax.dot_general(a, b, (dims, ((), ())), preferred_element_type=F32)


def column_plan(shard_size, context_size):
    rows = (D + FF) // shard_size
    blocks = rows // HEAD_DIM
    split = HEADS % blocks
    if rows % HEAD_DIM == 0 and split % context_size == 0 and (blocks - split) % context_size == 0:
        inner = [
            (at * HEAD_DIM, size * HEAD_DIM // context_size)
            for at, size in ((0, split), (split, blocks - split))
            if size
        ]
        segments = [(s * rows + at, width) for s in range(shard_size) for at, width in inner]
        return inner, segments
    return None, [(0, D // context_size), (D, FF // context_size)]


def take(array, segments, context, axis):
    parts = [
        lax.dynamic_slice_in_dim(array, base + context * width, width, axis)
        for base, width in segments
    ]
    return jnp.concatenate(parts, axis) if len(parts) > 1 else parts[0]


def untake(gathered, segments, axis):
    parts = []
    at = 0
    for _, width in segments:
        for c in range(gathered.shape[0]):
            parts.append(lax.slice_in_dim(gathered[c], at, at + width, axis=axis))
        at += width
    return jnp.concatenate(parts, axis)


def columns_kernel(n, parts, context_ref, in_ref, *out_refs):
    for c in range(n):

        @pl.when(context_ref[0] == c)
        def _():
            for out_ref, segments in zip(out_refs, parts):
                at = 0
                for base, width in segments:
                    out_ref[:, at : at + width] = in_ref[
                        :, base + c * width : base + (c + 1) * width
                    ]
                    at += width


def take_columns(array, parts, context, n):
    rows, columns = array.shape
    step = 32
    widths = [sum(width for _, width in segments) for segments in parts]
    return pl.pallas_call(
        functools.partial(columns_kernel, n, parts),
        grid_spec=pltpu.PrefetchScalarGridSpec(
            num_scalar_prefetch=1,
            grid=(rows // step,),
            in_specs=[pl.BlockSpec((step, columns), lambda i, context: (i, 0))],
            out_specs=[pl.BlockSpec((step, width), lambda i, context: (i, 0)) for width in widths],
        ),
        out_shape=[jax.ShapeDtypeStruct((rows, width), array.dtype) for width in widths],
        compiler_params=pltpu.CompilerParams(vmem_limit_bytes=14 * 2**20),
        cost_estimate=pl.CostEstimate(
            flops=0, bytes_accessed=2 * rows * (columns + sum(widths)), transcendentals=0
        ),
    )(context.reshape(1), array)


def rows_kernel(context_ref, in_ref, out_ref):
    out_ref[...] = in_ref[...]


def take_rows(array, segments, context):
    rows = sum(width for _, width in segments)
    columns = array.shape[1]
    step = HEAD_DIM

    def source(i, context):
        at, block = 0, 0
        for base, width in segments:
            block = jnp.where(
                i >= at // step, base // step + context[0] * (width // step) + i - at // step, block
            )
            at += width
        return (block, 0)

    return pl.pallas_call(
        rows_kernel,
        grid_spec=pltpu.PrefetchScalarGridSpec(
            num_scalar_prefetch=1,
            grid=(rows // step,),
            in_specs=[pl.BlockSpec((step, columns), source)],
            out_specs=pl.BlockSpec((step, columns), lambda i, context: (i, 0)),
        ),
        out_shape=jax.ShapeDtypeStruct((rows, columns), array.dtype),
        compiler_params=pltpu.CompilerParams(vmem_limit_bytes=8 * 2**20),
        cost_estimate=pl.CostEstimate(
            flops=0, bytes_accessed=4 * rows * columns, transcendentals=0
        ),
    )(context.reshape(1), array)


def join_kernel(places, *refs):
    *parts, out_ref, held, taken, given = refs
    copies, gives = [], []
    for i, (part, (row, column)) in enumerate(zip(parts, places)):
        where = (pl.ds(row, part.shape[0]), pl.ds(column, part.shape[1]))
        copies.append(pltpu.make_async_copy(part, held.at[where], taken.at[i]))
        gives.append(pltpu.make_async_copy(held.at[where], out_ref.at[where], given.at[i]))
    for copy in copies:
        copy.start()
    for copy, give in zip(copies, gives):
        copy.wait()
        give.start()
    for give in gives:
        give.wait()


def join(parts, places, shape):
    anywhere = pl.BlockSpec(memory_space=pl.ANY)
    return pl.pallas_call(
        functools.partial(join_kernel, places),
        in_specs=[anywhere] * len(parts),
        out_specs=anywhere,
        scratch_shapes=[
            pltpu.VMEM(shape, parts[0].dtype),
            pltpu.SemaphoreType.DMA((len(parts),)),
            pltpu.SemaphoreType.DMA((len(parts),)),
        ],
        out_shape=jax.ShapeDtypeStruct(shape, parts[0].dtype),
        compiler_params=pltpu.CompilerParams(vmem_limit_bytes=8 * 2**20),
        cost_estimate=pl.CostEstimate(
            flops=0, bytes_accessed=4 * shape[0] * shape[1], transcendentals=0
        ),
    )(*parts)


def lane_mask(shape, head):
    lane = lax.broadcasted_iota(jnp.int32, shape, len(shape) - 1)
    return (lane // HEAD_DIM) == head


def rotated(x, cosine, sine_low, sine_high):
    half = ROT // 2
    width = x.shape[1]
    return (
        x * cosine
        + pltpu.roll(x, width - half, 1) * sine_low
        + pltpu.roll(x, half, 1) * sine_high
    )


def stored(place_ref, p):
    return pl.ds(pl.multiple_of(place_ref[p] * BLK, BLK), BLK)


def attend_kernel(
    place_ref, q_main, k_main, v_main, q_rest, k_rest, v_rest, cos_ref, low_ref, high_ref,
    out_ref, total_ref, qr_ref, kr_ref, vr_ref, q_ref, k_ref, v_ref,
):
    tokens = q_ref.shape[0]
    for ref, main, rest in (
        (q_ref, q_main, q_rest), (k_ref, k_main, k_rest), (v_ref, v_main, v_rest)
    ):
        ref[: main.shape[0], :] = main[...]
        ref[main.shape[0] :, :] = rest[...]
    for p in range(tokens // BLK):
        here = pl.ds(p * BLK, BLK)
        there = stored(place_ref, p)
        cosine, low, high = cos_ref[there, :], low_ref[there, :], high_ref[there, :]
        query = rotated(q_ref[there, :], cosine, low, high).astype(BF16)
        qr_ref[here, :] = (query.astype(F32) * HEAD_DIM**-0.5).astype(BF16)
        kr_ref[here, :] = rotated(k_ref[there, :], cosine, low, high).astype(BF16)
        vr_ref[here, :] = v_ref[there, :].astype(BF16)
    for tile in range(tokens // TILE):
        first = tile * TILE // SEQ_LEN * SEQ_LEN
        last = (tile + 1) * TILE
        count = last - first
        query = qr_ref[pl.ds(tile * TILE, TILE), :]
        spans = [(tile * TILE, TILE)] + ([(first, count - TILE)] if count > TILE else [])
        keys = [kr_ref[pl.ds(*span), :] for span in spans]
        values = [vr_ref[pl.ds(*span), :] for span in spans]
        square = (TILE, TILE)
        allowed = lax.broadcasted_iota(jnp.int32, square, 1) <= lax.broadcasted_iota(
            jnp.int32, square, 0
        )
        outs, totals = [], []
        for head in range(2):
            mine = jnp.where(lane_mask(query.shape, head), query, jnp.zeros_like(query))
            scores = [dot(mine, part, ((1,), (1,))) for part in keys]
            scores[0] = jnp.where(allowed, scores[0], floor_score)
            highest = functools.reduce(
                jnp.maximum, [jnp.max(part, axis=1, keepdims=True) for part in scores]
            )
            weights = [jnp.exp(part - highest) for part in scores]
            total = sum(jnp.sum(part, axis=1, keepdims=True) for part in weights)
            out = sum(dot(part.astype(BF16), value) for part, value in zip(weights, values))
            outs.append(out / total)
            totals.append(highest + jnp.log(total))
        wide = (TILE, 2 * HEAD_DIM)
        first_head = lane_mask(wide, 0)
        out = jnp.where(first_head, outs[0], outs[1]).astype(BF16)
        total_ref[pl.ds(tile * TILE, TILE), :] = jnp.where(
            first_head, jnp.broadcast_to(totals[0], wide), jnp.broadcast_to(totals[1], wide)
        )
        for part in range(TILE // BLK):
            out_ref[stored(place_ref, tile * (TILE // BLK) + part), :] = out[
                part * BLK : (part + 1) * BLK
            ]


def attend_back_kernel(
    place_ref, q_ref, k_ref, v_ref, total_ref, out_ref, grad_ref, cos_ref, low_ref, high_ref,
    dq_ref, dk_ref, dv_ref, sums_ref, dq_acc, dk_acc, dv_acc,
):
    tokens = q_ref.shape[0]
    blocks = TILE // BLK
    dk_acc[...] = jnp.zeros_like(dk_acc)
    dv_acc[...] = jnp.zeros_like(dv_acc)
    for tile in range(tokens // TILE):
        first = tile * TILE // SEQ_LEN * SEQ_LEN
        last = (tile + 1) * TILE
        count = last - first
        places = [stored(place_ref, tile * blocks + part) for part in range(blocks)]
        query = q_ref[pl.ds(tile * TILE, TILE), :]
        keys = k_ref[pl.ds(first, count), :]
        values = v_ref[pl.ds(first, count), :]
        grad = jnp.concatenate([grad_ref[place, :] for place in places], 0)
        out = jnp.concatenate([out_ref[place, :] for place in places], 0)
        product = grad.astype(F32) * out.astype(F32)
        row = lax.broadcasted_iota(jnp.int32, (TILE, count), 0) + (tile * TILE - first)
        allowed = lax.broadcasted_iota(jnp.int32, (TILE, count), 1) <= row
        dq = jnp.zeros((TILE, 2 * HEAD_DIM), F32)
        for head in range(2):
            narrow = lane_mask(query.shape, head)
            mine = jnp.where(narrow, query, jnp.zeros_like(query))
            grad_mine = jnp.where(narrow, grad, jnp.zeros_like(grad))
            delta = jnp.sum(jnp.where(narrow, product, 0.0), axis=1, keepdims=True)
            total = total_ref[pl.ds(tile * TILE, TILE), pl.ds(head * HEAD_DIM, 1)]
            scores = jnp.where(allowed, dot(mine, keys, ((1,), (1,))), floor_score)
            weights = jnp.exp(scores - total)
            slope = dot(grad_mine, values, ((1,), (1,)))
            score_grad = (weights * (slope - delta)).astype(BF16)
            rounded = weights.astype(BF16)
            keys_mine = jnp.where(
                lane_mask(keys.shape, head), keys, jnp.zeros_like(keys)
            )
            dq = dq + dot(score_grad, keys_mine)
            dk_acc[pl.ds(first, count), :] += dot(score_grad, mine, ((0,), (0,)))
            dv_acc[pl.ds(first, count), :] += dot(rounded, grad_mine, ((0,), (0,)))
        dq_acc[pl.ds(tile * TILE, TILE), :] = dq * HEAD_DIM**-0.5
    sums = [jnp.zeros((1, 2 * HEAD_DIM), F32) for _ in range(3)]
    for p in range(tokens // BLK):
        here = pl.ds(p * BLK, BLK)
        there = stored(place_ref, p)
        cosine, low, high = cos_ref[there, :], -low_ref[there, :], -high_ref[there, :]
        for i, (acc, ref) in enumerate(((dq_acc, dq_ref), (dk_acc, dk_ref), (dv_acc, dv_ref))):
            part = acc[here, :]
            if i < 2:
                part = rotated(part, cosine, low, high)
            sums[i] = sums[i] + jnp.sum(part, axis=0, keepdims=True)
            ref[there, :] = part.astype(BF16)
    zero = jnp.zeros((5, 2 * HEAD_DIM), F32)
    sums_ref[...] = jnp.concatenate(sums + [zero], 0)


def attend(place, main, rest, tables, heads):
    tokens = main.shape[0] + rest.shape[0]
    pairs = heads // 2
    wide = 2 * HEAD_DIM

    def block(offset, rows=tokens):
        return pl.BlockSpec((rows, wide), lambda h, place: (0, h + offset))

    table = pl.BlockSpec((tokens, wide), lambda h, place: (0, 0))
    shape = (tokens, heads * HEAD_DIM)
    parts = [block(i * pairs, part.shape[0]) for part in (main, rest) for i in range(3)]
    return pl.pallas_call(
        attend_kernel,
        grid_spec=pltpu.PrefetchScalarGridSpec(
            num_scalar_prefetch=1,
            grid=(pairs,),
            in_specs=parts + [table, table, table],
            out_specs=[block(0)] * 5,
            scratch_shapes=[pltpu.VMEM((tokens, wide), F32)] * 3,
        ),
        out_shape=[
            jax.ShapeDtypeStruct(shape, BF16),
            jax.ShapeDtypeStruct(shape, F32),
            jax.ShapeDtypeStruct(shape, BF16),
            jax.ShapeDtypeStruct(shape, BF16),
            jax.ShapeDtypeStruct(shape, BF16),
        ],
        compiler_params=pltpu.CompilerParams(vmem_limit_bytes=28 * 2**20),
        cost_estimate=pl.CostEstimate(
            flops=8 * tokens * tokens * wide * pairs, bytes_accessed=30 * tokens * wide * pairs,
            transcendentals=tokens * tokens * heads,
        ),
    )(place, main, main, main, rest, rest, rest, *tables)


def attend_back(place, query, keys, values, total, out, grad, tables, heads):
    tokens = query.shape[0]
    pairs = heads // 2
    wide = 2 * HEAD_DIM
    block = pl.BlockSpec((tokens, wide), lambda h, place: (0, h))
    table = pl.BlockSpec((tokens, wide), lambda h, place: (0, 0))
    shape = jax.ShapeDtypeStruct((tokens, heads * HEAD_DIM), BF16)
    return pl.pallas_call(
        attend_back_kernel,
        grid_spec=pltpu.PrefetchScalarGridSpec(
            num_scalar_prefetch=1,
            grid=(pairs,),
            in_specs=[block] * 6 + [table] * 3,
            out_specs=[block] * 3 + [pl.BlockSpec((8, wide), lambda h, place: (0, h))],
            scratch_shapes=[pltpu.VMEM((tokens, wide), F32)] * 3,
        ),
        out_shape=[shape] * 3 + [jax.ShapeDtypeStruct((8, heads * HEAD_DIM), F32)],
        compiler_params=pltpu.CompilerParams(vmem_limit_bytes=48 * 2**20),
        cost_estimate=pl.CostEstimate(
            flops=20 * tokens * tokens * wide * pairs, bytes_accessed=30 * tokens * wide * pairs,
            transcendentals=tokens * tokens * heads,
        ),
    )(place, query, keys, values, total, out, grad, *tables)


def causal_blocks(assignment):
    count = assignment.shape[0]
    number = jnp.arange(count, dtype=jnp.int32)
    return jnp.sum(jnp.where(assignment[None, :] == number[:, None], number[None, :], 0), axis=1)


def group_positions(positions, assignment, context, group, turn):
    if group == SEQ_LEN:
        blocks_here = positions.shape[0] // BLK
        start = positions[0] - lax.dynamic_index_in_dim(
            assignment, context * blocks_here, 0, keepdims=False
        ) * BLK
        turned = jnp.roll(assignment, -turn * blocks_here)
        index = turned[:, None] * BLK + jnp.arange(BLK, dtype=jnp.int32)[None, :]
        return start + index.reshape(group)
    whole = lax.all_gather(positions, "context", axis=0, tiled=True)
    return jnp.roll(whole, -turn * positions.shape[0])


def rotary_tables(positions):
    half = ROT // 2
    lane = jnp.arange(2 * HEAD_DIM) % HEAD_DIM
    exponent = (lane % half).astype(F32)
    frequency = jnp.where(lane < ROT, 10000.0 ** (-2.0 * exponent / ROT), 0.0)
    angles = positions.astype(F32)[:, None] * frequency[None, :]
    cosine, sine = jnp.cos(angles), jnp.sin(angles)
    low = jnp.where(lane[None, :] < half, -sine, 0.0)
    high = jnp.where((lane[None, :] >= half) & (lane[None, :] < ROT), sine, 0.0)
    return cosine, low, high


def gelu_tanh(value):
    return jax.nn.gelu(value, approximate=True)


def tie(value, *after):
    return lax.optimization_barrier((value, after))[0] if after else value


def close(lines, *values):
    arrived, values = lax.optimization_barrier(([line.latest for line in lines], values))
    for line, arrays in zip(lines, arrived):
        line.latest = arrays
    return jax.tree.leaves(arrived) + jax.tree.leaves(values), values


class LineGather:
    def __init__(self, block):
        self.block, self.before, self.after = block, [], []

    def step(self, *after):
        n = lax.axis_size("context")
        t = len(self.before) + 1
        right, left = (self.before[-1], self.after[-1]) if t > 1 else (self.block, self.block)
        right, left = tie((right, left), *after)
        self.before.append(
            lax.ppermute(right, "context", [(a, a + 1) for a in range(t - 1, n - 1)])
        )
        self.after.append(lax.ppermute(left, "context", [(a, a - 1) for a in range(n - t, 0, -1)]))
        return self.before[-1], self.after[-1]

    @property
    def latest(self):
        return self.before[-1], self.after[-1]

    @latest.setter
    def latest(self, arrays):
        self.before[-1], self.after[-1] = arrays

    def rows(self, context, turn, first, count):
        n = lax.axis_size("context")
        before = self.before[::-1] + [self.block] + self.after
        missing = n - 1 - len(self.before)
        return place(context, turn, before, missing, first, count)

    def whole(self, context):
        n = lax.axis_size("context")
        return self.rows(context, jnp.zeros_like(context), 0, n)


class LineScatter:
    def __init__(self, partial, turn):
        self.partial, self.turn, self.steps = partial, turn, 0
        self.right = self.left = None

    def mine(self, j):
        n = lax.axis_size("context")
        rows = self.partial.shape[0] // n
        at = (jnp.clip(j, 0, n - 1) + n - self.turn) % n
        return lax.dynamic_slice_in_dim(self.partial, at * rows, rows, 0)

    def step(self, *after):
        n = lax.axis_size("context")
        context = lax.axis_index("context")
        self.steps = t = self.steps + 1
        right, left = self.mine(n - t + context), self.mine(context - (n - t))
        if t > 1:
            right = (right.astype(F32) + self.right.astype(F32)).astype(BF16)
            left = (left.astype(F32) + self.left.astype(F32)).astype(BF16)
        right, left = tie((right, left), *after)
        self.right = lax.ppermute(right, "context", [(a, a + 1) for a in range(t)])
        self.left = lax.ppermute(left, "context", [(n - 1 - a, n - 2 - a) for a in range(t)])
        return self.right, self.left

    @property
    def latest(self):
        return self.right, self.left

    @latest.setter
    def latest(self, arrays):
        self.right, self.left = arrays

    def result(self):
        own = self.mine(lax.axis_index("context")).astype(F32)
        return own + self.right.astype(F32) + self.left.astype(F32)


def place_kernel(n, missing, first, at_ref, *refs):
    *blocks, out_ref, held, taken, given = refs
    count, rows = held.shape[0], held.shape[1]

    def give(j):
        return pltpu.make_async_copy(
            held.at[j], out_ref.at[pl.ds(j * rows, rows), :], given.at[j]
        )

    def move(context, turn):
        copies = []
        for j in range(count):
            at = (turn + first + j) % n - context + n - 1 - missing
            if 0 <= at < len(blocks):
                copies.append((j, pltpu.make_async_copy(blocks[at], held.at[j], taken.at[j])))
        for _, copy in copies:
            copy.start()
        for j, copy in copies:
            copy.wait()
            give(j).start()
        for j, _ in copies:
            give(j).wait()

    for context in range(n):
        for turn in range(2):

            @pl.when((at_ref[0] == context) & (at_ref[1] == turn))
            def _():
                move(context, turn)


def place(context, turn, line, missing, first, count):
    n = (len(line) + 1) // 2 + missing
    rows, columns = line[0].shape
    anywhere = pl.BlockSpec(memory_space=pl.ANY)
    return pl.pallas_call(
        functools.partial(place_kernel, n, missing, first),
        grid_spec=pltpu.PrefetchScalarGridSpec(
            num_scalar_prefetch=1,
            grid=(1,),
            in_specs=[anywhere] * len(line),
            out_specs=anywhere,
            scratch_shapes=[
                pltpu.VMEM((count, rows, columns), line[0].dtype),
                pltpu.SemaphoreType.DMA((count,)),
                pltpu.SemaphoreType.DMA((count,)),
            ],
        ),
        out_shape=jax.ShapeDtypeStruct((count * rows, columns), line[0].dtype),
        compiler_params=pltpu.CompilerParams(vmem_limit_bytes=8 * 2**20),
        cost_estimate=pl.CostEstimate(
            flops=0, bytes_accessed=4 * count * rows * columns, transcendentals=0
        ),
    )(jnp.stack([context, turn]).astype(jnp.int32), *line)


def gather_shard(x):
    return lax.all_gather(x, "shard", axis=0, tiled=True)


def swap_sum(vector, axis):
    n = lax.axis_size(axis)
    if n & (n - 1):
        return lax.psum(vector, axis)
    k = 1
    while k < n:
        vector = vector + lax.ppermute(vector, axis, [(i, i ^ k) for i in range(n)])
        k *= 2
    return vector


def swap_gather(vector, axis):
    n = lax.axis_size(axis)
    if n & (n - 1):
        return lax.all_gather(vector, axis)
    here = lax.axis_index(axis)
    held = vector[None]
    k = 1
    while k < n:
        held = jnp.concatenate(
            [held, lax.ppermute(held, axis, [(i, i ^ k) for i in range(n)])], axis=0
        )
        k *= 2
    return jnp.stack([lax.dynamic_index_in_dim(held, j ^ here, 0, keepdims=False) for j in range(n)])


def scatter_shard(x):
    return lax.psum_scatter(x, "shard", scatter_dimension=0, tiled=True)


def spread_kernel(segments, in_ref, *refs):
    out_ref = refs[-1]
    for c in range(in_ref.shape[0]):
        part = in_ref[c].astype(F32)
        at = 0
        for base, width in segments:
            out_ref[:, base + c * width : base + (c + 1) * width] = part[:, at : at + width]
            at += width


def finish_hidden(parts, segments, rows, columns):
    n = parts.shape[0]
    step = 32
    return pl.pallas_call(
        functools.partial(spread_kernel, segments),
        grid=(rows // step,),
        in_specs=[pl.BlockSpec((n, step, parts.shape[2]), lambda i: (0, i, 0))],
        out_specs=pl.BlockSpec((step, columns), lambda i: (i, 0)),
        out_shape=jax.ShapeDtypeStruct((rows, columns), F32),
        compiler_params=pltpu.CompilerParams(vmem_limit_bytes=14 * 2**20),
        cost_estimate=pl.CostEstimate(
            flops=0, bytes_accessed=5 * rows * columns, transcendentals=0
        ),
    )(parts)


def finish_qkv(whole, parts, segments):
    n = parts.shape[0]
    rows = whole.shape[0]
    step = 32
    columns = n * sum(width for _, width in segments)
    return pl.pallas_call(
        functools.partial(spread_kernel, segments),
        grid=(rows // step,),
        in_specs=[
            pl.BlockSpec((n, step, parts.shape[2]), lambda i: (0, i, 0)),
            pl.BlockSpec(memory_space=pl.ANY),
        ],
        out_specs=pl.BlockSpec((step, columns), lambda i: (i, 0)),
        out_shape=jax.ShapeDtypeStruct(whole.shape, F32),
        input_output_aliases={1: 0},
        compiler_params=pltpu.CompilerParams(vmem_limit_bytes=14 * 2**20),
        cost_estimate=pl.CostEstimate(
            flops=0, bytes_accessed=6 * rows * columns, transcendentals=0
        ),
    )(parts, whole)


def finish_out_kernel(in_ref, out_ref):
    out_ref[...] = in_ref[0].astype(F32)


def finish_out(gathered, inner):
    n, rows, columns = gathered.shape
    step = HEAD_DIM
    bounds, at = [], 0
    for base, width in inner:
        bounds.append((base // step, width // step, at // step))
        at += width

    def source(b):
        c = first = 0
        for base, width, start in bounds:
            inside = b >= base
            c = jnp.where(inside, (b - base) // width, c)
            first = jnp.where(inside, start + (b - base) % width, first)
        return (c, first, 0)

    return pl.pallas_call(
        finish_out_kernel,
        grid=(n * rows // step,),
        in_specs=[pl.BlockSpec((1, step, columns), source)],
        out_specs=pl.BlockSpec((step, columns), lambda b: (b, 0)),
        out_shape=jax.ShapeDtypeStruct((n * rows, columns), F32),
        compiler_params=pltpu.CompilerParams(vmem_limit_bytes=8 * 2**20),
        cost_estimate=pl.CostEstimate(
            flops=0, bytes_accessed=6 * n * rows * columns, transcendentals=0
        ),
    )(gathered)


def local(
    block_input,
    input_weight,
    input_bias,
    output_weight,
    output_bias,
    norm_gain,
    norm_bias,
    assignment,
    positions,
    cotangent,
):
    tokens_here = block_input.shape[0]
    context_size = lax.axis_size("context")
    shard_size = lax.axis_size("shard")
    context = lax.axis_index("context")
    shard_here = lax.axis_index("shard")
    group = tokens_here * context_size
    heads = HEADS // context_size
    attn = heads * HEAD_DIM
    rows_here = input_weight.shape[0]
    steps = context_size - 1
    inner, segments = column_plan(shard_size, context_size)
    attn_segments = [(base, width) for base, width in segments if base < D]
    hidden_segments = [(base, width) for base, width in segments if base >= D]
    qkv_columns = [(base + i * D, width) for i in range(3) for base, width in attn_segments]
    hidden_columns = [(base + 2 * D, width) for base, width in hidden_segments]

    up = LineGather(cotangent.astype(BF16))
    up.step()

    small = jnp.concatenate(
        [input_bias, output_bias[0], output_bias[1], norm_gain, norm_bias], 0
    ).reshape(1, -1)
    small = gather_shard(small).astype(F32)
    cut = input_bias.shape[0]
    share = norm_gain.shape[0]
    bias_in = small[:, :cut].reshape(-1)
    bias_sum = (small[:, cut : cut + share] + small[:, cut + share : cut + 2 * share]).reshape(-1)
    gain = small[:, cut + 2 * share : cut + 3 * share].reshape(-1)
    shift = small[:, cut + 3 * share :].reshape(-1)

    centred = block_input - jnp.mean(block_input, axis=1, keepdims=True)
    inverse_std = lax.rsqrt(jnp.mean(centred * centred, axis=1, keepdims=True) + epsilon)
    normalized = centred * inverse_std
    normed_here = (normalized * gain + shift).astype(BF16)

    (in_part,) = take_columns(
        input_weight, [qkv_columns + hidden_columns], context, context_size
    )
    weight_in = gather_shard(in_part)
    weight_qkv, weight_hidden = weight_in[:, : 3 * attn], weight_in[:, 3 * attn :]
    out_part = take_rows(output_weight, inner, context) if inner is not None else output_weight
    gate, (normed_here,) = close([up], normed_here)
    weight_out = gather_shard(out_part)
    if inner is None:
        weight_out = take(weight_out, segments, context, 0)
    bias_qkv = take(bias_in, qkv_columns, context, 0)
    bias_hidden = take(bias_in, hidden_columns, context, 0)

    turn = (2 * context >= context_size).astype(jnp.int32)
    places = causal_blocks(jnp.roll(assignment, -turn * (tokens_here // BLK)))

    norm = LineGather(normed_here)
    for t in range(steps - 1):
        gate = norm.step(*gate)
        if t == 0:
            positions = tie(positions, *gate)
            tables = rotary_tables(
                group_positions(positions, assignment, context, group, turn)
            )

    normed_main = norm.rows(context, turn, 0, context_size - 1)
    norm.step()
    projected_main = dot(normed_main, weight_qkv) + bias_qkv
    hidden_main = dot(tie(normed_main, projected_main), weight_hidden) + bias_hidden
    active_main = gelu_tanh(hidden_main).astype(BF16)
    gate, (projected_main, active_main, hidden_main) = close(
        [norm], projected_main, active_main, hidden_main
    )
    normed_rest = norm.rows(context, turn, context_size - 1, 1)

    up.step(*gate)
    projected_rest = dot(normed_rest, weight_qkv) + bias_qkv
    attended, log_total, query, keys, values = attend(
        places, projected_main, projected_rest, tables, heads
    )
    gate, (attended, normed_rest) = close([up], attended, normed_rest)

    for t in range(steps - 2):
        up.step(*gate)
    hidden_rest = dot(normed_rest, weight_hidden) + bias_hidden
    active_rest = gelu_tanh(hidden_rest).astype(BF16)
    joined = join(
        [attended, active_main, active_rest],
        [(0, 0), (0, attn), (active_main.shape[0], attn)],
        (group, attn + active_main.shape[1]),
    )
    partial_out = dot(joined, weight_out).astype(BF16)
    gate, (partial_out, joined) = close([up], partial_out, joined)
    upstream = up.rows(context, turn, 0, context_size)

    out = LineScatter(partial_out, turn)
    out.step()
    out_grad = dot(joined, upstream, ((0,), (0,))).astype(BF16)
    gate, (out_grad, upstream) = close([out], out_grad, upstream)
    if inner is not None:
        out_grad_sum = scatter_shard(out_grad)

    out.step()
    cut = hidden_main.shape[0]
    hidden_rounded, hidden_sum = [], 0.0
    for pre, part in ((hidden_main, upstream[:cut]), (hidden_rest, upstream[cut:])):
        joined_grad = dot(part, weight_out[attn:], ((1,), (1,)))
        hidden_grad = jax.vjp(gelu_tanh, pre)[1](joined_grad)[0]
        hidden_rounded.append(hidden_grad.astype(BF16))
        hidden_sum = hidden_sum + jnp.sum(hidden_grad, axis=0)
    hidden_rounded = join(hidden_rounded, [(0, 0), (cut, 0)], (group, hidden_sum.shape[0]))
    normed = norm.rows(context, turn, 0, context_size)
    gate, (hidden_rounded, upstream, normed) = close([out], hidden_rounded, upstream, normed)

    for t in range(steps - 2):
        out.step()
    hidden_in_grad = dot(normed, hidden_rounded, ((0,), (0,))).astype(BF16)
    gate, (hidden_in_grad, hidden_rounded, upstream) = close(
        [out], hidden_in_grad, hidden_rounded, upstream
    )
    hidden_in_sum = scatter_shard(hidden_in_grad)
    block_output = block_input + out.result() + bias_sum

    attended_grad = dot(upstream, weight_out[:attn], ((1,), (1,))).astype(BF16)
    normed_grad = dot(hidden_rounded, weight_hidden, ((1,), (1,)))
    attended_grad, normed_grad = lax.optimization_barrier((attended_grad, normed_grad))

    gathers = []
    if inner is not None:
        gathers.append(LineGather(out_grad_sum))
        gathers[0].step(attended_grad)
    dq, dk, dv, sums = attend_back(
        places, query, keys, values, log_total, attended, attended_grad, tables, heads
    )
    qkv_rounded = join([dq, dk, dv], [(0, 0), (0, attn), (0, 2 * attn)], (group, 3 * attn))
    gate, (qkv_rounded,) = close(gathers, qkv_rounded)

    for gather in gathers:
        gather.step()
    qkv_in_grad = dot(normed, qkv_rounded, ((0,), (0,))).astype(BF16)
    gate, (qkv_in_grad, qkv_rounded, normed_grad) = close(
        gathers, qkv_in_grad, qkv_rounded, normed_grad
    )
    qkv_in_sum = scatter_shard(qkv_in_grad)

    for gather in gathers:
        for t in range(2, steps):
            gather.step()
    normed_grad = normed_grad + dot(qkv_rounded, weight_qkv, ((1,), (1,)))
    gain_sum = jnp.sum(normed_grad * ((normed.astype(F32) - shift) / gain), axis=0)
    shift_sum = jnp.sum(normed_grad, axis=0)
    partial_grad = normed_grad.astype(BF16)
    gate, (partial_grad, gain_sum, shift_sum) = close(gathers, partial_grad, gain_sum, shift_sum)
    grad = LineScatter(partial_grad, turn)

    hidden_gather, qkv_gather = LineGather(hidden_in_sum), LineGather(qkv_in_sum)
    done = ()
    if inner is not None:
        done = (
            finish_out(gathers[0].whole(context).reshape(context_size, -1, D), inner),
        )
    for t in range(steps):
        lines = [hidden_gather]
        hidden_gather.step(*gate)
        if t > 0:
            grad.step(*gate)
            lines.append(grad)
        gate, out = close(lines, *done)
        if done:
            (weight_out_grad,), done = out, ()

    for t in range(steps):
        qkv_gather.step(*gate)
        if grad.steps < steps:
            grad.step(*gate)
        done = ()
        if t == 1:
            hidden_parts = tie(hidden_gather.whole(context), *gate)
            done = (
                finish_hidden(
                    hidden_parts.reshape(context_size, rows_here, -1),
                    hidden_columns,
                    rows_here,
                    input_weight.shape[1],
                ),
            )
        gate, done = close([qkv_gather], *done)
        if done:
            (weight_in_grad,) = done
        if t == steps - 2:
            vectors = jnp.concatenate(
                [sums[0], sums[1], sums[2], hidden_sum, jnp.sum(cotangent, axis=0), gain_sum, shift_sum]
            )
            vectors = swap_gather(swap_sum(tie(vectors, *gate), "shard"), "context")
            columns = 3 * attn + hidden_sum.shape[0]
            bias_in_sum = untake(vectors[:, :columns], qkv_columns + hidden_columns, 0)
            others = jnp.sum(vectors[:, columns:], axis=0)

    if inner is None:
        whole = jnp.zeros((D + FF, D), BF16)
        at = 0
        for base, width in segments:
            whole = lax.dynamic_update_slice_in_dim(
                whole, out_grad[at : at + width], base + context * width, 0
            )
            at += width
        weight_out_grad = lax.psum(scatter_shard(whole), "context").astype(F32)
    qkv_parts = qkv_gather.whole(context).reshape(context_size, rows_here, -1)
    weight_in_grad = finish_qkv(weight_in_grad, qkv_parts, qkv_columns)

    def own_share(vector):
        length = vector.shape[0] // shard_size
        return lax.dynamic_slice_in_dim(vector, shard_here * length, length, 0)

    bias_row = own_share(others[:D])
    normed_grad = grad.result()
    scaled = normed_grad * gain
    input_grad = cotangent + inverse_std * (
        scaled
        - jnp.mean(scaled, axis=1, keepdims=True)
        - normalized * jnp.mean(scaled * normalized, axis=1, keepdims=True)
    )
    return (
        block_output,
        input_grad,
        weight_in_grad,
        own_share(bias_in_sum),
        weight_out_grad,
        jnp.stack([bias_row, bias_row]),
        own_share(others[D : 2 * D]),
        own_share(others[2 * D :]),
    )


def solution(mesh):
    return jax.shard_map(
        local,
        mesh=mesh,
        in_specs=(
            P(("shard", "context"), None),
            P("shard", None),
            P("shard"),
            P("shard", None),
            P(None, "shard"),
            P("shard"),
            P("shard"),
            P(),
            P(("shard", "context")),
            P(("shard", "context"), None),
        ),
        out_specs=(
            P(("shard", "context"), None),
            P(("shard", "context"), None),
            P("shard", None),
            P("shard"),
            P("shard", None),
            P(None, "shard"),
            P("shard"),
            P("shard"),
        ),
        check_vma=False,
    )
```

```python
import functools

import jax
import jax.numpy as jnp
from jax import lax
from jax.experimental import pallas as pl
from jax.experimental.pallas import tpu as pltpu
from jax.sharding import PartitionSpec as P

D = 2048
FF = 8192
HEADS = 32
HEAD_DIM = 64
ROT = 32
SEQ_LEN = 1024
BLK = 128
TILE = 256

epsilon = 1e-05
floor_score = -1e30

F32 = jnp.float32
BF16 = jnp.bfloat16


def dot(a, b, dims=((1,), (0,))):
    return lax.dot_general(a, b, (dims, ((), ())), preferred_element_type=F32)


def column_plan(shard_size, context_size):
    rows = (D + FF) // shard_size
    blocks = rows // HEAD_DIM
    split = HEADS % blocks
    if rows % HEAD_DIM == 0 and split % context_size == 0 and (blocks - split) % context_size == 0:
        inner = [
            (at * HEAD_DIM, size * HEAD_DIM // context_size)
            for at, size in ((0, split), (split, blocks - split))
            if size
        ]
        segments = [(s * rows + at, width) for s in range(shard_size) for at, width in inner]
        return inner, segments
    return None, [(0, D // context_size), (D, FF // context_size)]


def take(array, segments, context, axis):
    parts = [
        lax.dynamic_slice_in_dim(array, base + context * width, width, axis)
        for base, width in segments
    ]
    return jnp.concatenate(parts, axis) if len(parts) > 1 else parts[0]


def untake(gathered, segments, axis):
    parts = []
    at = 0
    for _, width in segments:
        for c in range(gathered.shape[0]):
            parts.append(lax.slice_in_dim(gathered[c], at, at + width, axis=axis))
        at += width
    return jnp.concatenate(parts, axis)


def columns_kernel(n, parts, context_ref, in_ref, *out_refs):
    for c in range(n):

        @pl.when(context_ref[0] == c)
        def _():
            for out_ref, segments in zip(out_refs, parts):
                at = 0
                for base, width in segments:
                    out_ref[:, at : at + width] = in_ref[
                        :, base + c * width : base + (c + 1) * width
                    ]
                    at += width


def take_columns(array, parts, context, n):
    rows, columns = array.shape
    step = 32
    widths = [sum(width for _, width in segments) for segments in parts]
    return pl.pallas_call(
        functools.partial(columns_kernel, n, parts),
        grid_spec=pltpu.PrefetchScalarGridSpec(
            num_scalar_prefetch=1,
            grid=(rows // step,),
            in_specs=[pl.BlockSpec((step, columns), lambda i, context: (i, 0))],
            out_specs=[pl.BlockSpec((step, width), lambda i, context: (i, 0)) for width in widths],
        ),
        out_shape=[jax.ShapeDtypeStruct((rows, width), array.dtype) for width in widths],
        compiler_params=pltpu.CompilerParams(vmem_limit_bytes=14 * 2**20),
        cost_estimate=pl.CostEstimate(
            flops=0, bytes_accessed=2 * rows * (columns + sum(widths)), transcendentals=0
        ),
    )(context.reshape(1), array)


def rows_kernel(context_ref, in_ref, out_ref):
    out_ref[...] = in_ref[...]


def take_rows(array, segments, context):
    rows = sum(width for _, width in segments)
    columns = array.shape[1]
    step = HEAD_DIM

    def source(i, context):
        at, block = 0, 0
        for base, width in segments:
            block = jnp.where(
                i >= at // step, base // step + context[0] * (width // step) + i - at // step, block
            )
            at += width
        return (block, 0)

    return pl.pallas_call(
        rows_kernel,
        grid_spec=pltpu.PrefetchScalarGridSpec(
            num_scalar_prefetch=1,
            grid=(rows // step,),
            in_specs=[pl.BlockSpec((step, columns), source)],
            out_specs=pl.BlockSpec((step, columns), lambda i, context: (i, 0)),
        ),
        out_shape=jax.ShapeDtypeStruct((rows, columns), array.dtype),
        compiler_params=pltpu.CompilerParams(vmem_limit_bytes=8 * 2**20),
        cost_estimate=pl.CostEstimate(
            flops=0, bytes_accessed=4 * rows * columns, transcendentals=0
        ),
    )(context.reshape(1), array)


def join_kernel(places, *refs):
    *parts, out_ref, held, taken, given = refs
    copies, gives = [], []
    for i, (part, (row, column)) in enumerate(zip(parts, places)):
        where = (pl.ds(row, part.shape[0]), pl.ds(column, part.shape[1]))
        copies.append(pltpu.make_async_copy(part, held.at[where], taken.at[i]))
        gives.append(pltpu.make_async_copy(held.at[where], out_ref.at[where], given.at[i]))
    for copy in copies:
        copy.start()
    for copy, give in zip(copies, gives):
        copy.wait()
        give.start()
    for give in gives:
        give.wait()


def join(parts, places, shape):
    anywhere = pl.BlockSpec(memory_space=pl.ANY)
    return pl.pallas_call(
        functools.partial(join_kernel, places),
        in_specs=[anywhere] * len(parts),
        out_specs=anywhere,
        scratch_shapes=[
            pltpu.VMEM(shape, parts[0].dtype),
            pltpu.SemaphoreType.DMA((len(parts),)),
            pltpu.SemaphoreType.DMA((len(parts),)),
        ],
        out_shape=jax.ShapeDtypeStruct(shape, parts[0].dtype),
        compiler_params=pltpu.CompilerParams(vmem_limit_bytes=8 * 2**20),
        cost_estimate=pl.CostEstimate(
            flops=0, bytes_accessed=4 * shape[0] * shape[1], transcendentals=0
        ),
    )(*parts)


def lane_mask(shape, head):
    lane = lax.broadcasted_iota(jnp.int32, shape, len(shape) - 1)
    return (lane // HEAD_DIM) == head


def rotated(x, cosine, sine_low, sine_high):
    half = ROT // 2
    width = x.shape[1]
    return (
        x * cosine
        + pltpu.roll(x, width - half, 1) * sine_low
        + pltpu.roll(x, half, 1) * sine_high
    )


def stored(place_ref, p):
    return pl.ds(pl.multiple_of(place_ref[p] * BLK, BLK), BLK)


def attend_kernel(
    place_ref, q_main, k_main, v_main, q_rest, k_rest, v_rest, cos_ref, low_ref, high_ref,
    out_ref, total_ref, qr_ref, kr_ref, vr_ref, q_ref, k_ref, v_ref,
):
    tokens = q_ref.shape[0]
    for ref, main, rest in (
        (q_ref, q_main, q_rest), (k_ref, k_main, k_rest), (v_ref, v_main, v_rest)
    ):
        ref[: main.shape[0], :] = main[...]
        ref[main.shape[0] :, :] = rest[...]
    for p in range(tokens // BLK):
        here = pl.ds(p * BLK, BLK)
        there = stored(place_ref, p)
        cosine, low, high = cos_ref[there, :], low_ref[there, :], high_ref[there, :]
        query = rotated(q_ref[there, :], cosine, low, high).astype(BF16)
        qr_ref[here, :] = (query.astype(F32) * HEAD_DIM**-0.5).astype(BF16)
        kr_ref[here, :] = rotated(k_ref[there, :], cosine, low, high).astype(BF16)
        vr_ref[here, :] = v_ref[there, :].astype(BF16)
    for tile in range(tokens // TILE):
        first = tile * TILE // SEQ_LEN * SEQ_LEN
        last = (tile + 1) * TILE
        count = last - first
        query = qr_ref[pl.ds(tile * TILE, TILE), :]
        spans = [(tile * TILE, TILE)] + ([(first, count - TILE)] if count > TILE else [])
        keys = [kr_ref[pl.ds(*span), :] for span in spans]
        values = [vr_ref[pl.ds(*span), :] for span in spans]
        square = (TILE, TILE)
        allowed = lax.broadcasted_iota(jnp.int32, square, 1) <= lax.broadcasted_iota(
            jnp.int32, square, 0
        )
        outs, totals = [], []
        for head in range(2):
            mine = jnp.where(lane_mask(query.shape, head), query, jnp.zeros_like(query))
            scores = [dot(mine, part, ((1,), (1,))) for part in keys]
            scores[0] = jnp.where(allowed, scores[0], floor_score)
            highest = functools.reduce(
                jnp.maximum, [jnp.max(part, axis=1, keepdims=True) for part in scores]
            )
            weights = [jnp.exp(part - highest) for part in scores]
            total = sum(jnp.sum(part, axis=1, keepdims=True) for part in weights)
            out = sum(dot(part.astype(BF16), value) for part, value in zip(weights, values))
            outs.append(out / total)
            totals.append(highest + jnp.log(total))
        wide = (TILE, 2 * HEAD_DIM)
        first_head = lane_mask(wide, 0)
        out = jnp.where(first_head, outs[0], outs[1]).astype(BF16)
        total_ref[pl.ds(tile * TILE, TILE), :] = jnp.where(
            first_head, jnp.broadcast_to(totals[0], wide), jnp.broadcast_to(totals[1], wide)
        )
        for part in range(TILE // BLK):
            out_ref[stored(place_ref, tile * (TILE // BLK) + part), :] = out[
                part * BLK : (part + 1) * BLK
            ]


def attend_back_kernel(
    place_ref, q_ref, k_ref, v_ref, total_ref, out_ref, grad_ref, cos_ref, low_ref, high_ref,
    dq_ref, dk_ref, dv_ref, sums_ref, dq_acc, dk_acc, dv_acc,
):
    tokens = q_ref.shape[0]
    blocks = TILE // BLK
    dk_acc[...] = jnp.zeros_like(dk_acc)
    dv_acc[...] = jnp.zeros_like(dv_acc)
    for tile in range(tokens // TILE):
        first = tile * TILE // SEQ_LEN * SEQ_LEN
        last = (tile + 1) * TILE
        count = last - first
        places = [stored(place_ref, tile * blocks + part) for part in range(blocks)]
        query = q_ref[pl.ds(tile * TILE, TILE), :]
        keys = k_ref[pl.ds(first, count), :]
        values = v_ref[pl.ds(first, count), :]
        grad = jnp.concatenate([grad_ref[place, :] for place in places], 0)
        out = jnp.concatenate([out_ref[place, :] for place in places], 0)
        product = grad.astype(F32) * out.astype(F32)
        row = lax.broadcasted_iota(jnp.int32, (TILE, count), 0) + (tile * TILE - first)
        allowed = lax.broadcasted_iota(jnp.int32, (TILE, count), 1) <= row
        dq = jnp.zeros((TILE, 2 * HEAD_DIM), F32)
        for head in range(2):
            narrow = lane_mask(query.shape, head)
            mine = jnp.where(narrow, query, jnp.zeros_like(query))
            grad_mine = jnp.where(narrow, grad, jnp.zeros_like(grad))
            delta = jnp.sum(jnp.where(narrow, product, 0.0), axis=1, keepdims=True)
            total = total_ref[pl.ds(tile * TILE, TILE), pl.ds(head * HEAD_DIM, 1)]
            scores = jnp.where(allowed, dot(mine, keys, ((1,), (1,))), floor_score)
            weights = jnp.exp(scores - total)
            slope = dot(grad_mine, values, ((1,), (1,)))
            score_grad = (weights * (slope - delta)).astype(BF16)
            rounded = weights.astype(BF16)
            keys_mine = jnp.where(
                lane_mask(keys.shape, head), keys, jnp.zeros_like(keys)
            )
            dq = dq + dot(score_grad, keys_mine)
            dk_acc[pl.ds(first, count), :] += dot(score_grad, mine, ((0,), (0,)))
            dv_acc[pl.ds(first, count), :] += dot(rounded, grad_mine, ((0,), (0,)))
        dq_acc[pl.ds(tile * TILE, TILE), :] = dq * HEAD_DIM**-0.5
    sums = [jnp.zeros((1, 2 * HEAD_DIM), F32) for _ in range(3)]
    for p in range(tokens // BLK):
        here = pl.ds(p * BLK, BLK)
        there = stored(place_ref, p)
        cosine, low, high = cos_ref[there, :], -low_ref[there, :], -high_ref[there, :]
        for i, (acc, ref) in enumerate(((dq_acc, dq_ref), (dk_acc, dk_ref), (dv_acc, dv_ref))):
            part = acc[here, :]
            if i < 2:
                part = rotated(part, cosine, low, high)
            sums[i] = sums[i] + jnp.sum(part, axis=0, keepdims=True)
            ref[there, :] = part.astype(BF16)
    zero = jnp.zeros((5, 2 * HEAD_DIM), F32)
    sums_ref[...] = jnp.concatenate(sums + [zero], 0)


def attend(place, main, rest, tables, heads):
    tokens = main.shape[0] + rest.shape[0]
    pairs = heads // 2
    wide = 2 * HEAD_DIM

    def block(offset, rows=tokens):
        return pl.BlockSpec((rows, wide), lambda h, place: (0, h + offset))

    table = pl.BlockSpec((tokens, wide), lambda h, place: (0, 0))
    shape = (tokens, heads * HEAD_DIM)
    parts = [block(i * pairs, part.shape[0]) for part in (main, rest) for i in range(3)]
    return pl.pallas_call(
        attend_kernel,
        grid_spec=pltpu.PrefetchScalarGridSpec(
            num_scalar_prefetch=1,
            grid=(pairs,),
            in_specs=parts + [table, table, table],
            out_specs=[block(0)] * 5,
            scratch_shapes=[pltpu.VMEM((tokens, wide), F32)] * 3,
        ),
        out_shape=[
            jax.ShapeDtypeStruct(shape, BF16),
            jax.ShapeDtypeStruct(shape, F32),
            jax.ShapeDtypeStruct(shape, BF16),
            jax.ShapeDtypeStruct(shape, BF16),
            jax.ShapeDtypeStruct(shape, BF16),
        ],
        compiler_params=pltpu.CompilerParams(vmem_limit_bytes=28 * 2**20),
        cost_estimate=pl.CostEstimate(
            flops=8 * tokens * tokens * wide * pairs, bytes_accessed=30 * tokens * wide * pairs,
            transcendentals=tokens * tokens * heads,
        ),
    )(place, main, main, main, rest, rest, rest, *tables)


def attend_back(place, query, keys, values, total, out, grad, tables, heads):
    tokens = query.shape[0]
    pairs = heads // 2
    wide = 2 * HEAD_DIM
    block = pl.BlockSpec((tokens, wide), lambda h, place: (0, h))
    table = pl.BlockSpec((tokens, wide), lambda h, place: (0, 0))
    shape = jax.ShapeDtypeStruct((tokens, heads * HEAD_DIM), BF16)
    return pl.pallas_call(
        attend_back_kernel,
        grid_spec=pltpu.PrefetchScalarGridSpec(
            num_scalar_prefetch=1,
            grid=(pairs,),
            in_specs=[block] * 6 + [table] * 3,
            out_specs=[block] * 3 + [pl.BlockSpec((8, wide), lambda h, place: (0, h))],
            scratch_shapes=[pltpu.VMEM((tokens, wide), F32)] * 3,
        ),
        out_shape=[shape] * 3 + [jax.ShapeDtypeStruct((8, heads * HEAD_DIM), F32)],
        compiler_params=pltpu.CompilerParams(vmem_limit_bytes=48 * 2**20),
        cost_estimate=pl.CostEstimate(
            flops=20 * tokens * tokens * wide * pairs, bytes_accessed=30 * tokens * wide * pairs,
            transcendentals=tokens * tokens * heads,
        ),
    )(place, query, keys, values, total, out, grad, *tables)


def causal_blocks(assignment):
    count = assignment.shape[0]
    number = jnp.arange(count, dtype=jnp.int32)
    return jnp.sum(jnp.where(assignment[None, :] == number[:, None], number[None, :], 0), axis=1)


def group_positions(positions, assignment, context, group, turn):
    if group == SEQ_LEN:
        blocks_here = positions.shape[0] // BLK
        start = positions[0] - lax.dynamic_index_in_dim(
            assignment, context * blocks_here, 0, keepdims=False
        ) * BLK
        turned = jnp.roll(assignment, -turn * blocks_here)
        index = turned[:, None] * BLK + jnp.arange(BLK, dtype=jnp.int32)[None, :]
        return start + index.reshape(group)
    whole = lax.all_gather(positions, "context", axis=0, tiled=True)
    return jnp.roll(whole, -turn * positions.shape[0])


def rotary_tables(positions):
    half = ROT // 2
    lane = jnp.arange(2 * HEAD_DIM) % HEAD_DIM
    exponent = (lane % half).astype(F32)
    frequency = jnp.where(lane < ROT, 10000.0 ** (-2.0 * exponent / ROT), 0.0)
    angles = positions.astype(F32)[:, None] * frequency[None, :]
    cosine, sine = jnp.cos(angles), jnp.sin(angles)
    low = jnp.where(lane[None, :] < half, -sine, 0.0)
    high = jnp.where((lane[None, :] >= half) & (lane[None, :] < ROT), sine, 0.0)
    return cosine, low, high


def gelu_tanh(value):
    return jax.nn.gelu(value, approximate=True)


def tie(value, *after):
    return lax.optimization_barrier((value, after))[0] if after else value


def close(lines, *values):
    arrived, values = lax.optimization_barrier(([line.latest for line in lines], values))
    for line, arrays in zip(lines, arrived):
        line.latest = arrays
    return jax.tree.leaves(arrived) + jax.tree.leaves(values), values


class LineGather:
    def __init__(self, block):
        self.block, self.before, self.after = block, [], []

    def step(self, *after):
        n = lax.axis_size("context")
        t = len(self.before) + 1
        right, left = (self.before[-1], self.after[-1]) if t > 1 else (self.block, self.block)
        right, left = tie((right, left), *after)
        self.before.append(
            lax.ppermute(right, "context", [(a, a + 1) for a in range(t - 1, n - 1)])
        )
        self.after.append(lax.ppermute(left, "context", [(a, a - 1) for a in range(n - t, 0, -1)]))
        return self.before[-1], self.after[-1]

    @property
    def latest(self):
        return self.before[-1], self.after[-1]

    @latest.setter
    def latest(self, arrays):
        self.before[-1], self.after[-1] = arrays

    def rows(self, context, turn, first, count):
        n = lax.axis_size("context")
        before = self.before[::-1] + [self.block] + self.after
        missing = n - 1 - len(self.before)
        return place(context, turn, before, missing, first, count)

    def whole(self, context):
        n = lax.axis_size("context")
        return self.rows(context, jnp.zeros_like(context), 0, n)


class LineScatter:
    def __init__(self, partial, turn):
        self.partial, self.turn, self.steps = partial, turn, 0
        self.right = self.left = None

    def mine(self, j):
        n = lax.axis_size("context")
        rows = self.partial.shape[0] // n
        at = (jnp.clip(j, 0, n - 1) + n - self.turn) % n
        return lax.dynamic_slice_in_dim(self.partial, at * rows, rows, 0)

    def step(self, *after):
        n = lax.axis_size("context")
        context = lax.axis_index("context")
        self.steps = t = self.steps + 1
        right, left = self.mine(n - t + context), self.mine(context - (n - t))
        if t > 1:
            right = (right.astype(F32) + self.right.astype(F32)).astype(BF16)
            left = (left.astype(F32) + self.left.astype(F32)).astype(BF16)
        right, left = tie((right, left), *after)
        self.right = lax.ppermute(right, "context", [(a, a + 1) for a in range(t)])
        self.left = lax.ppermute(left, "context", [(n - 1 - a, n - 2 - a) for a in range(t)])
        return self.right, self.left

    @property
    def latest(self):
        return self.right, self.left

    @latest.setter
    def latest(self, arrays):
        self.right, self.left = arrays

    def result(self):
        own = self.mine(lax.axis_index("context")).astype(F32)
        return own + self.right.astype(F32) + self.left.astype(F32)


def place_kernel(n, missing, first, at_ref, *refs):
    *blocks, out_ref, held, taken, given = refs
    count, rows = held.shape[0], held.shape[1]

    def give(j):
        return pltpu.make_async_copy(
            held.at[j], out_ref.at[pl.ds(j * rows, rows), :], given.at[j]
        )

    def move(context, turn):
        copies = []
        for j in range(count):
            at = (turn + first + j) % n - context + n - 1 - missing
            if 0 <= at < len(blocks):
                copies.append((j, pltpu.make_async_copy(blocks[at], held.at[j], taken.at[j])))
        for _, copy in copies:
            copy.start()
        for j, copy in copies:
            copy.wait()
            give(j).start()
        for j, _ in copies:
            give(j).wait()

    for context in range(n):
        for turn in range(2):

            @pl.when((at_ref[0] == context) & (at_ref[1] == turn))
            def _():
                move(context, turn)


def place(context, turn, line, missing, first, count):
    n = (len(line) + 1) // 2 + missing
    rows, columns = line[0].shape
    anywhere = pl.BlockSpec(memory_space=pl.ANY)
    return pl.pallas_call(
        functools.partial(place_kernel, n, missing, first),
        grid_spec=pltpu.PrefetchScalarGridSpec(
            num_scalar_prefetch=1,
            grid=(1,),
            in_specs=[anywhere] * len(line),
            out_specs=anywhere,
            scratch_shapes=[
                pltpu.VMEM((count, rows, columns), line[0].dtype),
                pltpu.SemaphoreType.DMA((count,)),
                pltpu.SemaphoreType.DMA((count,)),
            ],
        ),
        out_shape=jax.ShapeDtypeStruct((count * rows, columns), line[0].dtype),
        compiler_params=pltpu.CompilerParams(vmem_limit_bytes=8 * 2**20),
        cost_estimate=pl.CostEstimate(
            flops=0, bytes_accessed=4 * count * rows * columns, transcendentals=0
        ),
    )(jnp.stack([context, turn]).astype(jnp.int32), *line)


def gather_shard(x):
    return lax.all_gather(x, "shard", axis=0, tiled=True)


def swap_sum(vector, axis):
    n = lax.axis_size(axis)
    if n & (n - 1):
        return lax.psum(vector, axis)
    k = 1
    while k < n:
        vector = vector + lax.ppermute(vector, axis, [(i, i ^ k) for i in range(n)])
        k *= 2
    return vector


def swap_gather(vector, axis):
    n = lax.axis_size(axis)
    if n & (n - 1):
        return lax.all_gather(vector, axis)
    here = lax.axis_index(axis)
    held = vector[None]
    k = 1
    while k < n:
        held = jnp.concatenate(
            [held, lax.ppermute(held, axis, [(i, i ^ k) for i in range(n)])], axis=0
        )
        k *= 2
    return jnp.stack([lax.dynamic_index_in_dim(held, j ^ here, 0, keepdims=False) for j in range(n)])


def scatter_shard(x):
    return lax.psum_scatter(x, "shard", scatter_dimension=0, tiled=True)


def spread_kernel(segments, in_ref, *refs):
    out_ref = refs[-1]
    for c in range(in_ref.shape[0]):
        part = in_ref[c].astype(F32)
        at = 0
        for base, width in segments:
            out_ref[:, base + c * width : base + (c + 1) * width] = part[:, at : at + width]
            at += width


def finish_hidden(parts, segments, rows, columns):
    n = parts.shape[0]
    step = 32
    return pl.pallas_call(
        functools.partial(spread_kernel, segments),
        grid=(rows // step,),
        in_specs=[pl.BlockSpec((n, step, parts.shape[2]), lambda i: (0, i, 0))],
        out_specs=pl.BlockSpec((step, columns), lambda i: (i, 0)),
        out_shape=jax.ShapeDtypeStruct((rows, columns), F32),
        compiler_params=pltpu.CompilerParams(vmem_limit_bytes=14 * 2**20),
        cost_estimate=pl.CostEstimate(
            flops=0, bytes_accessed=5 * rows * columns, transcendentals=0
        ),
    )(parts)


def finish_qkv(whole, parts, segments):
    n = parts.shape[0]
    rows = whole.shape[0]
    step = 32
    columns = n * sum(width for _, width in segments)
    return pl.pallas_call(
        functools.partial(spread_kernel, segments),
        grid=(rows // step,),
        in_specs=[
            pl.BlockSpec((n, step, parts.shape[2]), lambda i: (0, i, 0)),
            pl.BlockSpec(memory_space=pl.ANY),
        ],
        out_specs=pl.BlockSpec((step, columns), lambda i: (i, 0)),
        out_shape=jax.ShapeDtypeStruct(whole.shape, F32),
        input_output_aliases={1: 0},
        compiler_params=pltpu.CompilerParams(vmem_limit_bytes=14 * 2**20),
        cost_estimate=pl.CostEstimate(
            flops=0, bytes_accessed=6 * rows * columns, transcendentals=0
        ),
    )(parts, whole)


def finish_out_kernel(in_ref, out_ref):
    out_ref[...] = in_ref[0].astype(F32)


def finish_out(gathered, inner):
    n, rows, columns = gathered.shape
    step = HEAD_DIM
    bounds, at = [], 0
    for base, width in inner:
        bounds.append((base // step, width // step, at // step))
        at += width

    def source(b):
        c = first = 0
        for base, width, start in bounds:
            inside = b >= base
            c = jnp.where(inside, (b - base) // width, c)
            first = jnp.where(inside, start + (b - base) % width, first)
        return (c, first, 0)

    return pl.pallas_call(
        finish_out_kernel,
        grid=(n * rows // step,),
        in_specs=[pl.BlockSpec((1, step, columns), source)],
        out_specs=pl.BlockSpec((step, columns), lambda b: (b, 0)),
        out_shape=jax.ShapeDtypeStruct((n * rows, columns), F32),
        compiler_params=pltpu.CompilerParams(vmem_limit_bytes=8 * 2**20),
        cost_estimate=pl.CostEstimate(
            flops=0, bytes_accessed=6 * n * rows * columns, transcendentals=0
        ),
    )(gathered)


def local(
    block_input,
    input_weight,
    input_bias,
    output_weight,
    output_bias,
    norm_gain,
    norm_bias,
    assignment,
    positions,
    cotangent,
):
    tokens_here = block_input.shape[0]
    context_size = lax.axis_size("context")
    shard_size = lax.axis_size("shard")
    context = lax.axis_index("context")
    shard_here = lax.axis_index("shard")
    group = tokens_here * context_size
    heads = HEADS // context_size
    attn = heads * HEAD_DIM
    rows_here = input_weight.shape[0]
    steps = context_size - 1
    inner, segments = column_plan(shard_size, context_size)
    attn_segments = [(base, width) for base, width in segments if base < D]
    hidden_segments = [(base, width) for base, width in segments if base >= D]
    qkv_columns = [(base + i * D, width) for i in range(3) for base, width in attn_segments]
    hidden_columns = [(base + 2 * D, width) for base, width in hidden_segments]

    up = LineGather(cotangent.astype(BF16))
    up.step()

    small = jnp.concatenate(
        [input_bias, output_bias[0], output_bias[1], norm_gain, norm_bias], 0
    ).reshape(1, -1)
    small = gather_shard(small).astype(F32)
    cut = input_bias.shape[0]
    share = norm_gain.shape[0]
    bias_in = small[:, :cut].reshape(-1)
    bias_sum = (small[:, cut : cut + share] + small[:, cut + share : cut + 2 * share]).reshape(-1)
    gain = small[:, cut + 2 * share : cut + 3 * share].reshape(-1)
    shift = small[:, cut + 3 * share :].reshape(-1)

    centred = block_input - jnp.mean(block_input, axis=1, keepdims=True)
    inverse_std = lax.rsqrt(jnp.mean(centred * centred, axis=1, keepdims=True) + epsilon)
    normalized = centred * inverse_std
    normed_here = (normalized * gain + shift).astype(BF16)

    (in_part,) = take_columns(
        input_weight, [qkv_columns + hidden_columns], context, context_size
    )
    weight_in = gather_shard(in_part)
    weight_qkv, weight_hidden = weight_in[:, : 3 * attn], weight_in[:, 3 * attn :]
    gate, (normed_here, output_weight) = close([up], normed_here, output_weight)
    out_part = take_rows(output_weight, inner, context) if inner is not None else output_weight
    weight_out = gather_shard(out_part)
    if inner is None:
        weight_out = take(weight_out, segments, context, 0)
    bias_qkv = take(bias_in, qkv_columns, context, 0)
    bias_hidden = take(bias_in, hidden_columns, context, 0)

    turn = (2 * context >= context_size).astype(jnp.int32)
    places = causal_blocks(jnp.roll(assignment, -turn * (tokens_here // BLK)))

    norm = LineGather(normed_here)
    for t in range(steps - 1):
        gate = norm.step(*gate)
        if t == 0:
            positions = tie(positions, *gate)
            tables = rotary_tables(
                group_positions(positions, assignment, context, group, turn)
            )

    normed_main = norm.rows(context, turn, 0, context_size - 1)
    norm.step()
    projected_main = dot(normed_main, weight_qkv) + bias_qkv
    hidden_main = dot(tie(normed_main, projected_main), weight_hidden) + bias_hidden
    active_main = gelu_tanh(hidden_main).astype(BF16)
    gate, (projected_main, active_main, hidden_main) = close(
        [norm], projected_main, active_main, hidden_main
    )
    normed_rest = norm.rows(context, turn, context_size - 1, 1)

    up.step(*gate)
    projected_rest = dot(normed_rest, weight_qkv) + bias_qkv
    attended, log_total, query, keys, values = attend(
        places, projected_main, projected_rest, tables, heads
    )
    gate, (attended, normed_rest) = close([up], attended, normed_rest)

    for t in range(steps - 2):
        up.step(*gate)
    hidden_rest = dot(normed_rest, weight_hidden) + bias_hidden
    active_rest = gelu_tanh(hidden_rest).astype(BF16)
    joined = join(
        [attended, active_main, active_rest],
        [(0, 0), (0, attn), (active_main.shape[0], attn)],
        (group, attn + active_main.shape[1]),
    )
    partial_out = dot(joined, weight_out).astype(BF16)
    gate, (partial_out, joined) = close([up], partial_out, joined)
    upstream = up.rows(context, turn, 0, context_size)

    out = LineScatter(partial_out, turn)
    out.step()
    out_grad = dot(joined, upstream, ((0,), (0,))).astype(BF16)
    gate, (out_grad, upstream) = close([out], out_grad, upstream)
    if inner is not None:
        out_grad_sum = scatter_shard(out_grad)

    out.step()
    cut = hidden_main.shape[0]
    hidden_rounded, hidden_sum = [], 0.0
    for pre, part in ((hidden_main, upstream[:cut]), (hidden_rest, upstream[cut:])):
        joined_grad = dot(part, weight_out[attn:], ((1,), (1,)))
        hidden_grad = jax.vjp(gelu_tanh, pre)[1](joined_grad)[0]
        hidden_rounded.append(hidden_grad.astype(BF16))
        hidden_sum = hidden_sum + jnp.sum(hidden_grad, axis=0)
    hidden_rounded = join(hidden_rounded, [(0, 0), (cut, 0)], (group, hidden_sum.shape[0]))
    normed = norm.rows(context, turn, 0, context_size)
    gate, (hidden_rounded, upstream, normed) = close([out], hidden_rounded, upstream, normed)

    for t in range(steps - 2):
        out.step()
    hidden_in_grad = dot(normed, hidden_rounded, ((0,), (0,))).astype(BF16)
    gate, (hidden_in_grad, hidden_rounded, upstream) = close(
        [out], hidden_in_grad, hidden_rounded, upstream
    )
    hidden_in_sum = scatter_shard(hidden_in_grad)
    block_output = block_input + out.result() + bias_sum

    attended_grad = dot(upstream, weight_out[:attn], ((1,), (1,))).astype(BF16)
    normed_grad = dot(hidden_rounded, weight_hidden, ((1,), (1,)))
    attended_grad, normed_grad = lax.optimization_barrier((attended_grad, normed_grad))

    gathers = []
    if inner is not None:
        gathers.append(LineGather(out_grad_sum))
        gathers[0].step(attended_grad)
    dq, dk, dv, sums = attend_back(
        places, query, keys, values, log_total, attended, attended_grad, tables, heads
    )
    qkv_rounded = join([dq, dk, dv], [(0, 0), (0, attn), (0, 2 * attn)], (group, 3 * attn))
    gate, (qkv_rounded,) = close(gathers, qkv_rounded)

    for gather in gathers:
        gather.step()
    qkv_in_grad = dot(normed, qkv_rounded, ((0,), (0,))).astype(BF16)
    gate, (qkv_in_grad, qkv_rounded, normed_grad) = close(
        gathers, qkv_in_grad, qkv_rounded, normed_grad
    )
    qkv_in_sum = scatter_shard(qkv_in_grad)

    for gather in gathers:
        for t in range(2, steps):
            gather.step()
    normed_grad = normed_grad + dot(qkv_rounded, weight_qkv, ((1,), (1,)))
    gain_sum = jnp.sum(normed_grad * ((normed.astype(F32) - shift) / gain), axis=0)
    shift_sum = jnp.sum(normed_grad, axis=0)
    partial_grad = normed_grad.astype(BF16)
    gate, (partial_grad, gain_sum, shift_sum) = close(gathers, partial_grad, gain_sum, shift_sum)
    grad = LineScatter(partial_grad, turn)

    hidden_gather, qkv_gather = LineGather(hidden_in_sum), LineGather(qkv_in_sum)
    done = ()
    if inner is not None:
        done = (
            finish_out(gathers[0].whole(context).reshape(context_size, -1, D), inner),
        )
    for t in range(steps):
        lines = [hidden_gather]
        hidden_gather.step(*gate)
        if t > 0:
            grad.step(*gate)
            lines.append(grad)
        gate, out = close(lines, *done)
        if done:
            (weight_out_grad,), done = out, ()

    for t in range(steps):
        qkv_gather.step(*gate)
        if grad.steps < steps:
            grad.step(*gate)
        done = ()
        if t == 1:
            hidden_parts = tie(hidden_gather.whole(context), *gate)
            done = (
                finish_hidden(
                    hidden_parts.reshape(context_size, rows_here, -1),
                    hidden_columns,
                    rows_here,
                    input_weight.shape[1],
                ),
            )
        gate, done = close([qkv_gather], *done)
        if done:
            (weight_in_grad,) = done
        if t == steps - 2:
            vectors = jnp.concatenate(
                [sums[0], sums[1], sums[2], hidden_sum, jnp.sum(cotangent, axis=0), gain_sum, shift_sum]
            )
            vectors = swap_gather(swap_sum(tie(vectors, *gate), "shard"), "context")
            columns = 3 * attn + hidden_sum.shape[0]
            bias_in_sum = untake(vectors[:, :columns], qkv_columns + hidden_columns, 0)
            others = jnp.sum(vectors[:, columns:], axis=0)

    if inner is None:
        whole = jnp.zeros((D + FF, D), BF16)
        at = 0
        for base, width in segments:
            whole = lax.dynamic_update_slice_in_dim(
                whole, out_grad[at : at + width], base + context * width, 0
            )
            at += width
        weight_out_grad = lax.psum(scatter_shard(whole), "context").astype(F32)
    qkv_parts = qkv_gather.whole(context).reshape(context_size, rows_here, -1)
    weight_in_grad = finish_qkv(weight_in_grad, qkv_parts, qkv_columns)

    def own_share(vector):
        length = vector.shape[0] // shard_size
        return lax.dynamic_slice_in_dim(vector, shard_here * length, length, 0)

    bias_row = own_share(others[:D])
    normed_grad = grad.result()
    scaled = normed_grad * gain
    input_grad = cotangent + inverse_std * (
        scaled
        - jnp.mean(scaled, axis=1, keepdims=True)
        - normalized * jnp.mean(scaled * normalized, axis=1, keepdims=True)
    )
    return (
        block_output,
        input_grad,
        weight_in_grad,
        own_share(bias_in_sum),
        weight_out_grad,
        jnp.stack([bias_row, bias_row]),
        own_share(others[D : 2 * D]),
        own_share(others[2 * D :]),
    )


def solution(mesh):
    return jax.shard_map(
        local,
        mesh=mesh,
        in_specs=(
            P(("shard", "context"), None),
            P("shard", None),
            P("shard"),
            P("shard", None),
            P(None, "shard"),
            P("shard"),
            P("shard"),
            P(),
            P(("shard", "context")),
            P(("shard", "context"), None),
        ),
        out_specs=(
            P(("shard", "context"), None),
            P(("shard", "context"), None),
            P("shard", None),
            P("shard"),
            P("shard", None),
            P(None, "shard"),
            P("shard"),
            P("shard"),
        ),
        check_vma=False,
    )
```
